256 devices in a mesh: group: 8 (over x, core), sub: 32 (over y, z).
Axes of the slice: x: 4, y: 4, z: 8, core: 2. Of those that a mesh axis runs over, the one named last changes fastest.
Arguments:
- resid_iface: float32 [256, 16, 4352], P(('group', 'sub')), may hold values from -6 to 6
- resid_inner: float32 [256, 16, 3072], P(('group', 'sub')), may hold values from -6 to 6
- weights: float32 [256, 4352], P(('group', 'sub')), may hold values from 0.25 to 0.75
- nbr: int32 [256, 32], P(('group', 'sub')), may hold values from 0 to 1, as said below
- own2: int32 [256, 128], P(('group', 'sub')), may hold values from 0 to 2047
- cidx: int32 [256, 8], P(('group', 'sub')), may hold values from 0 to 16
- neumann: bfloat16 [256, 17, 256, 256], P(('group', 'sub'))
- dirichlet: bfloat16 [256, 8, 384, 384], P(('group', 'sub'))
- coupling: bfloat16 [256, 8, 256, 384], P(('group', 'sub')), may hold values from -0.375 to 0.375
- coarse_basis: bfloat16 [256, 4352, 128], P(('group', 'sub')), may hold values from -0.5 to 0.5
- group_basis: float32 [16384, 512], P(('group', 'sub')), may hold values from -0.25 to 0.25
- group_inverse: float32 [16384, 2048], P('group', 'sub'), as said below
- top_inverse: float32 [512, 512], replicated, as said below
Outputs:
- interface_out: float32 [256, 16, 4352], P(('group', 'sub'))
- interior_out: float32 [256, 16, 3072], P(('group', 'sub'))
The draws below stay inside these ranges and needn't reach their ends.
Inputs may be any that keep to these rules, and one draw needn't show every extreme that they name: Symmetric within each group (nbr[(g, q), j] = nbr[(g, j), q]) with nbr[(g, q), q] = 0. `group_inverse`: each matrix of a group is symmetric. `top_inverse`: symmetric.
All inputs are finite; a program needn't handle non-finite values.
Results may differ from the reference program's by a relative error of at most 0.013.
Values may be sent and summed in bfloat16 or wider, within the bound.
A program may use at most 64 MiB of HBM per device.

```python
import math
import jax
import jax.numpy as jnp
from jax import lax

R = 16
BI = 384
BN = 256
KI = 8
NC = 128
NC2 = 2048
NC3 = 512
GROUPS = 8
SUBS = 32
SUBDOMAINS = 256
FB = 128
SLOTS = 34
NB = 4352
KN = 17
NI = 3072


def dominant(key, lead, order, diag, spread):
    first, second = jax.random.split(key)
    shape = lead + (order, order)
    noise = jax.random.normal(first, shape, jnp.float32)
    diag_scale = jax.random.uniform(second, lead + (order,), jnp.float32, 0.7, 1.3)
    sym = (noise + jnp.swapaxes(noise, -1, -2)) * (spread / math.sqrt(2.0 * order))
    return sym + jnp.eye(order, dtype=jnp.float32) * (diag * diag_scale)[..., None]


def draw_nbr(key, part):
    picks = jax.random.randint(key, (GROUPS, SUBS, SUBS), 0, 20)
    chosen = (picks < 9).astype(jnp.int32)
    rows = jnp.arange(SUBS, dtype=jnp.int32)[:, None]
    cols = jnp.arange(SUBS, dtype=jnp.int32)[None, :]
    upper = chosen * (rows < cols).astype(jnp.int32)[None, :, :]
    return (upper + jnp.swapaxes(upper, 1, 2)).reshape(SUBDOMAINS, SUBS)


def draw_neumann(key, part):
    blocks = dominant(key, (SUBDOMAINS, KN), BN, 1.0, 0.25)
    return blocks.astype(jnp.bfloat16)


def draw_dirichlet(key, part):
    blocks = dominant(key, (SUBDOMAINS, KI), BI, 1.0, 0.25)
    return blocks.astype(jnp.bfloat16)


def draw_group_inverse(key, part):
    blocks = dominant(key, (GROUPS,), NC2, 1.0, 0.25)
    return blocks.reshape(GROUPS * NC2, NC2)


def draw_top_inverse(key, part):
    level = math.sqrt(NC3 / (GROUPS * NC2))
    return dominant(key, (), NC3, level, 0.25 * level)


def touch_ends(drawn, key, low, top_value):
    place = [jax.random.randint(jax.random.fold_in(key, axis), (), 0, length) for axis, length in enumerate(drawn.shape)]
    main_axis = drawn.shape.index(max(drawn.shape))
    next_to = place[:main_axis] + [(place[main_axis] + 1) % drawn.shape[main_axis]] + place[main_axis + 1:]
    return drawn.at[tuple(place)].set(low).at[tuple(next_to)].set(top_value)


def steps_of(key, extent, cuts, low, top_value):
    factor_of = 1.0
    for dim, parts in cuts:
        steps = jax.random.uniform(jax.random.fold_in(jax.random.fold_in(key, 6), dim), (parts,), jnp.float32, low / len(cuts), top_value / len(cuts))
        factor_of = factor_of * jnp.repeat(jnp.exp(steps), extent[dim] // parts).reshape((-1,) + (1,) * (len(extent) - 1 - dim))
    return factor_of


def gaussian(own_key, shape, scale, reach, cuts=(), kind=jnp.bfloat16):
    entries = jax.random.normal(own_key, shape, jnp.float32) * scale
    if len(cuts) > 0:
        entries = steps_of(own_key, shape, cuts, -0.22, 0.18) * entries
    return jnp.clip(entries, min=-reach, max=reach).astype(kind)


def setup_inputs(seed: int = 0) -> dict:
    keys = jax.random.split(jax.random.key(seed), 14)
    return {
        "resid_iface": gaussian(keys[0], (SUBDOMAINS, R, NB), 1.0, 6.0, ((0, 256),), jnp.float32),
        "resid_inner": gaussian(keys[1], (SUBDOMAINS, R, NI), 1.0, 6.0, ((0, 256),), jnp.float32),
        "weights": jnp.clip(0.25 + 0.5 * jax.random.uniform(keys[2], (SUBDOMAINS, NB), jnp.float32) ** steps_of(keys[2], (SUBDOMAINS, NB), ((0, 256),), -0.2, 0.2), 0.25, 0.75),
        "nbr": draw_nbr(jax.random.fold_in(keys[13], 71), 0),
        "own2": touch_ends(jax.random.randint(keys[4], (SUBDOMAINS, NC), 0, NC2), jax.random.fold_in(keys[4], 1), 0, NC2 - 1).astype(jnp.int32),
        "cidx": touch_ends(jax.random.randint(keys[5], (SUBDOMAINS, KI), 0, KN), jax.random.fold_in(keys[5], 1), 0, KN - 1).astype(jnp.int32),
        "neumann": draw_neumann(jax.random.fold_in(keys[13], 71), 0),
        "dirichlet": draw_dirichlet(jax.random.fold_in(keys[13], 71), 0),
        "coupling": gaussian(keys[8], (SUBDOMAINS, KI, BN, BI), BN ** -0.5, 0.375, ((0, 256),)),
        "coarse_basis": gaussian(keys[9], (SUBDOMAINS, NB, NC), ((NB * NC) ** -0.25), 0.5, ((0, 256),)),
        "group_basis": gaussian(keys[10], (GROUPS * NC2, NC3), NC3 ** -0.5, 0.25, ((0, 256),), jnp.float32),
        "group_inverse": draw_group_inverse(jax.random.fold_in(keys[13], 71), 0),
        "top_inverse": draw_top_inverse(jax.random.fold_in(keys[13], 71), 0),
    }


def reference(resid_iface, resid_inner, weights, nbr, own2, cidx, neumann, dirichlet, coupling, coarse_basis, group_basis, group_inverse, top_inverse):
    highest = lax.Precision.HIGHEST
    slot_mask = jnp.concatenate([nbr.astype(jnp.float32), jnp.ones((SUBDOMAINS, 2), jnp.float32)], axis=1)
    scale = jnp.repeat(slot_mask, FB, axis=1) * weights

    def local_first(items):
        resid, factor, basis, blocks, owners = items
        weighted = (factor[None, :] * resid).astype(jnp.bfloat16)
        local0 = jnp.dot(weighted.astype(jnp.float32), basis.astype(jnp.float32), precision=highest)
        onehot = (owners[:, None] == jnp.arange(NC2, dtype=jnp.int32)[None, :]).astype(jnp.float32)
        contrib = jnp.dot(local0, onehot, precision=highest)
        neumann_part = jnp.einsum("rkb,kbc->rkc", weighted.reshape(R, KN, BN).astype(jnp.float32), blocks.astype(jnp.float32)).reshape(R, NB)
        return contrib, neumann_part

    contrib, neumann_part = lax.map(local_first, (resid_iface, scale, coarse_basis, neumann, own2))
    level2 = contrib.reshape(GROUPS, SUBS, R, NC2).sum(axis=1)
    basis2 = group_basis.reshape(GROUPS, NC2, NC3)
    level3 = jnp.einsum("grc,gcd->rd", level2, basis2, precision=highest)
    coarse3 = jnp.dot(level3, top_inverse, precision=highest)
    inverse2 = group_inverse.reshape(GROUPS, NC2, NC2)
    coarse2 = jnp.einsum("grc,gcd->grd", level2, inverse2, precision=highest) + jnp.einsum("rd,gcd->grc", coarse3, basis2, precision=highest)
    coarse2 = coarse2.astype(jnp.bfloat16)
    coarse_each = jnp.repeat(coarse2, SUBS, axis=0)

    def local_second(items):
        coarse_row, owners, basis, part, factor = items
        values = jnp.take(coarse_row, owners, axis=1)
        spread = lax.dot_general(values.astype(jnp.float32), basis.astype(jnp.float32), (((1,), (1,)), ((), ())), precision=highest)
        return factor[None, :] * (part + spread)

    scaled = lax.map(local_second, (coarse_each, own2, coarse_basis, neumann_part, scale))
    slots = scaled.reshape(GROUPS, SUBS, R, SLOTS, FB)
    inner = slots[:, :, :, :SUBS, :]
    received = jnp.swapaxes(inner, 1, 3)
    lower_face = slots[:, :, :, SUBS, :]
    upper_face = slots[:, :, :, SUBS + 1, :]
    zero_face = jnp.zeros_like(lower_face[:1])
    from_below = jnp.concatenate([zero_face, upper_face[:-1]], axis=0)
    from_above = jnp.concatenate([lower_face[1:], zero_face], axis=0)
    total = jnp.concatenate([inner + received, (lower_face + from_below)[:, :, :, None, :], (upper_face + from_above)[:, :, :, None, :]], axis=3)
    interface_out = total.reshape(SUBDOMAINS, R, NB)

    def local_third(items):
        iface_row, inner_row, picks, links, blocks = items
        iface_blocks = iface_row.reshape(R, KN, BN).astype(jnp.bfloat16)
        picked = jnp.take(iface_blocks, picks, axis=1)
        pushed = jnp.einsum("rkb,kbc->rkc", picked.astype(jnp.float32), links.astype(jnp.float32))
        inner_rhs = (inner_row.reshape(R, KI, BI) - pushed).astype(jnp.bfloat16)
        return jnp.einsum("rkb,kbc->rkc", inner_rhs.astype(jnp.float32), blocks.astype(jnp.float32)).reshape(R, NI)

    interior_out = lax.map(local_third, (interface_out, resid_inner, cidx, coupling, dirichlet))
    return interface_out, interior_out
```

```python
import functools

import jax
import jax.numpy as jnp
from jax import lax
from jax.experimental import pallas as pl
from jax.experimental.pallas import tpu as pltpu
from jax.sharding import PartitionSpec as P

F32 = jnp.float32
BF16 = jnp.bfloat16
MESH = pl.DeviceIdType.MESH
NT = (((1,), (1,)), ((), ()))

NY, NZ = 4, 8


def dot(a, b):
    return jnp.dot(a, b, preferred_element_type=F32)


def dot_nt(a, b):
    return lax.dot_general(a, b, NT, preferred_element_type=F32)


def kernel(
    ngroup,
    nsub,
    resid_h,
    inner_h,
    weights_h,
    nbr_h,
    own_h,
    cidx_h,
    neumann_h,
    dirichlet_h,
    coupling_h,
    cb_h,
    basis_h,
    ginv_h,
    top_h,
    iface_h,
    inter_h,
    resid,
    inner,
    weights,
    nbr,
    cidx,
    neumann,
    dirichlet,
    coupling,
    cb,
    basis,
    ginv,
    top,
    scale,
    weighted,
    loc_all,
    own_all,
    bsend,
    bpk,
    bfull,
    ohl,
    hmask,
    lhs,
    lev,
    ohv,
    ginv_pad,
    nt_pad,
    p2,
    p3,
    c2,
    nsc,
    scaled,
    dsend,
    drecv,
    face,
    picked,
    iface,
    inter,
    in_sem,
    out_sem,
    send_sem,
    recv_sem,
):
    g = lax.axis_index("group")
    sub = lax.axis_index("sub")
    y, z = sub // NZ, sub % NZ
    par = sub % 2
    slots = nsub + 2
    kn = neumann.shape[0]
    ki = dirichlet.shape[0]
    bi = dirichlet.shape[1]

    loads = [
        (nbr_h, nbr),
        (weights_h, weights),
        (resid_h, resid),
        (cb_h, cb),
        (own_h, own_all.at[sub]),
        (basis_h, basis),
        (neumann_h, neumann),
        (top_h, top),
        (ginv_h, ginv),
        (cidx_h, cidx),
        (inner_h, inner),
        (coupling_h, coupling),
        (dirichlet_h, dirichlet),
    ]
    loads = [pltpu.make_async_copy(s, d, in_sem.at[i]) for i, (s, d) in enumerate(loads)]
    (ld_nbr, ld_w, ld_resid, ld_cb, ld_own, ld_basis, ld_neu, ld_top, ld_ginv, ld_cidx, ld_inner, ld_coup, ld_dir) = loads
    for ld in loads:
        ld.start()

    barrier = pltpu.get_barrier_semaphore()

    def greet_sub(o, _):
        pl.semaphore_signal(barrier, inc=1, device_id=(g, (sub + o) % nsub), device_id_type=MESH)
        return 0

    def greet_group(o, _):
        pl.semaphore_signal(barrier, inc=1, device_id=((g + o) % ngroup, sub), device_id_type=MESH)
        return 0

    lax.fori_loop(1, nsub, greet_sub, 0)
    lax.fori_loop(1, ngroup, greet_group, 0)

    def rcopy(src, dst, phase, tg, ts):
        return pltpu.make_async_remote_copy(
            src_ref=src,
            dst_ref=dst,
            send_sem=send_sem.at[phase],
            recv_sem=recv_sem.at[phase],
            device_id=(tg, ts),
            device_id_type=MESH,
        )

    def wait_recv(ref, phase):
        pltpu.make_async_copy(ref, ref, recv_sem.at[phase]).wait()

    def wait_send(ref, phase):
        pltpu.make_async_copy(ref, ref, send_sem.at[phase]).wait()

    def send_sub(buf, phase):
        def step(o, _):
            ts = ((y + o // NZ) % NY) * NZ + (z + o) % NZ
            rcopy(buf.at[sub], buf.at[sub], phase, g, ts).start()
            return 0

        lax.fori_loop(1, nsub, step, 0)

    lane = lax.broadcasted_iota(jnp.int32, (1, 128), 1)
    low = lane < 64
    ld_nbr.wait()
    ld_w.wait()
    ld_resid.wait()
    for j in range(slots):
        sl = pl.ds(128 * j, 128)
        sc = weights[:, sl]
        if j < nsub:
            sc = sc * nbr[0, j].astype(F32)
        scale[j] = sc
        weighted[:, sl] = (sc * resid[:, sl]).astype(BF16)
    ld_cb.wait()
    loc_all[sub] = dot(weighted[...], cb[...]).astype(BF16)

    ld_basis.wait()
    for k in range(NZ):
        t = pl.ds(128 * (k // 2), 128)
        a, b = basis[:32, t], basis[32:, t]
        if k % 2 == 0:
            pk = jnp.where(low, a, pltpu.roll(b, 64, 1))
        else:
            pk = jnp.where(low, pltpu.roll(a, 64, 1), b)
        bsend[k] = pk.astype(BF16)
    bpk[sub] = bsend[z]
    ld_own.wait()

    pl.semaphore_wait(barrier, nsub - 1 + ngroup - 1)

    send_sub(loc_all, 0)

    def send_z(o, _):
        tz = (z + o) % NZ
        rcopy(own_all.at[sub], own_all.at[sub], 1, g, y * NZ + tz).start()
        rcopy(bsend.at[tz], bpk.at[sub], 2, g, y * NZ + tz).start()
        return 0

    lax.fori_loop(1, NZ, send_z, 0)
    rows = pl.ds(pl.multiple_of(y * NZ, NZ), NZ)
    wait_recv(own_all.at[pl.ds(0, NZ - 1)], 1)
    wait_recv(bpk.at[pl.ds(0, NZ - 1)], 2)

    def send_y(o, _):
        ts = ((y + o) % NY) * NZ + z
        rcopy(own_all.at[rows], own_all.at[rows], 3, g, ts).start()
        rcopy(bpk.at[rows], bpk.at[rows], 4, g, ts).start()
        return 0

    lax.fori_loop(1, NY, send_y, 0)

    ld_top.wait()
    nt = dot(basis[...].astype(BF16), top[...].astype(BF16))
    mine_rows = pl.ds(pl.multiple_of(par * 64, 64), 64)
    other_rows = pl.ds(pl.multiple_of((1 - par) * 64, 64), 64)
    for k in range(NZ):
        v = nt[:, 128 * (k // 2) : 128 * (k // 2) + 128]
        if k % 2:
            v = pltpu.roll(v, 64, 1)
        nt_pad[mine_rows, pl.ds(128 * k, 128)] = jnp.where(low, v, 0.0).astype(BF16)
    nt_pad[other_rows, :] = jnp.zeros((64, 128 * NZ), BF16)
    ld_ginv.wait()
    ginv_pad[mine_rows, :] = ginv[...].astype(BF16)
    ginv_pad[other_rows, :] = jnp.zeros((64, ginv.shape[1]), BF16)

    wait_recv(own_all.at[pl.ds(0, nsub - NZ)], 3)

    def masks(s, _):
        o = own_all[s]
        lo, hi = o & 255, o >> 8
        ohl[:, pl.ds(pl.multiple_of(s * 128, 128), 128)] = (
            (lax.broadcasted_iota(jnp.int32, (256, 128), 0) == lo).astype(F32).astype(BF16)
        )
        for h in range(8):
            m = (hi == h).astype(F32)
            hmask[s, pl.ds(16 * h, 16), :] = jnp.broadcast_to(m, (16, 128)).astype(BF16)
        return 0

    lax.fori_loop(0, nsub, masks, 0)

    wait_recv(bpk.at[pl.ds(0, nsub - NZ)], 4)

    def unpack(q, _):
        p = bpk[q].astype(F32)
        at = pl.multiple_of(q * 64, 64)
        bfull[pl.ds(at, 32), :] = jnp.where(low, p, 0.0).astype(BF16)
        bfull[pl.ds(at + 32, 32), :] = jnp.where(low, pltpu.roll(p, 64, 1), 0.0).astype(BF16)
        return 0

    lax.fori_loop(0, nsub, unpack, 0)

    wait_recv(loc_all.at[pl.ds(0, nsub - 1)], 0)
    for s in range(nsub):
        v = loc_all[s]
        for h in range(8):
            lhs[pl.ds(16 * h, 16), pl.ds(128 * s, 128)] = v * hmask[s, pl.ds(16 * h, 16), :]
    level2 = dot_nt(lhs[...], ohl[...])
    for h in range(8):
        lev[:, pl.ds(256 * h, 256)] = level2[16 * h : 16 * h + 16, :].astype(BF16)
    p2[g] = dot(lev[...], bfull[...]).astype(BF16)

    def send_group(o, _):
        rcopy(p2.at[g], p2.at[g], 5, (g + o) % ngroup, sub).start()
        return 0

    lax.fori_loop(1, ngroup, send_group, 0)
    solved = dot_nt(lev[...], ginv_pad[...])
    wait_recv(p2.at[pl.ds(0, ngroup - 1)], 5)
    level3 = p2[0].astype(F32)
    for k in range(1, ngroup):
        level3 = level3 + p2[k].astype(F32)
    p3[z] = level3.astype(BF16)

    def send_top(o, _):
        rcopy(p3.at[z], p3.at[z], 6, g, y * NZ + (z + o) % NZ).start()
        return 0

    lax.fori_loop(1, NZ, send_top, 0)

    def pick(t, _):
        at = pl.multiple_of(t * 256, 256)
        ohv[pl.ds(at, 256), :] = (
            (lax.broadcasted_iota(jnp.int32, (256, 128), 0) + at == own_all[sub]).astype(F32).astype(BF16)
        )
        return 0

    lax.fori_loop(0, 8, pick, 0)

    wait_recv(p3.at[pl.ds(0, NZ - 1)], 6)
    lifted = dot_nt(jnp.concatenate([p3[k] for k in range(NZ)], axis=1), nt_pad[...])
    c2[sub] = (solved + lifted).astype(BF16)

    send_sub(c2, 7)
    ld_neu.wait()
    for k in range(kn):
        v = dot(weighted[:, 256 * k : 256 * k + 256], neumann[k])
        nsc[2 * k] = v[:, :128] * scale[2 * k]
        nsc[2 * k + 1] = v[:, 128:] * scale[2 * k + 1]
    wait_recv(c2.at[pl.ds(0, nsub - 1)], 7)
    coarse2 = jnp.concatenate([c2[2 * t] + c2[2 * t + 1] for t in range(nsub // 2)], axis=1)
    values = dot(coarse2, ohv[...]).astype(BF16)

    spread = dot_nt(values, cb[pl.ds(128 * nsub, 256), :])
    for i in range(2):
        scaled[nsub + i] = nsc[nsub + i] + scale[nsub + i] * spread[:, 128 * i : 128 * i + 128]

    to_upper = rcopy(scaled.at[nsub + 1], face.at[0], 8, jnp.minimum(g + 1, ngroup - 1), sub)
    to_lower = rcopy(scaled.at[nsub], face.at[1], 9, jnp.maximum(g - 1, 0), sub)

    @pl.when(g < ngroup - 1)
    def _():
        to_upper.start()

    @pl.when(g > 0)
    def _():
        to_lower.start()

    for c in range(NY):
        ty = (y + 1 + c) % NY
        first = ty * NZ
        spread = dot_nt(values, cb[pl.ds(pl.multiple_of(first * 128, 1024), 1024), :])
        for i in range(NZ):
            v = nsc[first + i] + scale[first + i] * spread[:, 128 * i : 128 * i + 128]
            scaled[first + i] = v
            dsend[first + i] = v.astype(BF16)

        def send_slot(o, _):
            to = first + (z + o) % NZ
            rcopy(dsend.at[to], drecv.at[sub], 10, g, to).start()
            return 0

        lax.fori_loop(0 if c < NY - 1 else 1, NZ, send_slot, 0)
    drecv[sub] = dsend[sub]

    @pl.when(g > 0)
    def _():
        to_upper.wait_recv()

    @pl.when(g == 0)
    def _():
        face[0] = jnp.zeros(face.shape[1:], F32)

    @pl.when(g < ngroup - 1)
    def _():
        to_lower.wait_recv()

    @pl.when(g == ngroup - 1)
    def _():
        face[1] = jnp.zeros(face.shape[1:], F32)

    ld_cidx.wait()
    ld_inner.wait()
    ld_coup.wait()
    ld_dir.wait()
    wait_recv(drecv.at[pl.ds(0, nsub - 1)], 10)
    for j in range(slots):
        got = drecv[j].astype(F32) if j < nsub else face[j - nsub]
        v = scaled[j] + got
        iface[:, pl.ds(128 * j, 128)] = v
        picked[j] = v.astype(BF16)
    st_iface = pltpu.make_async_copy(iface, iface_h, out_sem.at[0])
    st_iface.start()
    for k in range(ki):
        at = 2 * cidx[0, k]
        block = jnp.concatenate([picked[at], picked[at + 1]], axis=1)
        sl = pl.ds(bi * k, bi)
        rhs = (inner[:, sl] - dot(block, coupling[k])).astype(BF16)
        inter[:, sl] = dot(rhs, dirichlet[k])
    st_inter = pltpu.make_async_copy(inter, inter_h, out_sem.at[1])
    st_inter.start()

    wait_send(loc_all.at[pl.ds(0, nsub - 1)], 0)
    wait_send(own_all.at[pl.ds(0, NZ - 1)], 1)
    wait_send(bpk.at[pl.ds(0, NZ - 1)], 2)
    wait_send(own_all.at[pl.ds(0, nsub - NZ)], 3)
    wait_send(bpk.at[pl.ds(0, nsub - NZ)], 4)
    wait_send(p2.at[pl.ds(0, ngroup - 1)], 5)
    wait_send(p3.at[pl.ds(0, NZ - 1)], 6)
    wait_send(c2.at[pl.ds(0, nsub - 1)], 7)

    @pl.when(g < ngroup - 1)
    def _():
        to_upper.wait_send()

    @pl.when(g > 0)
    def _():
        to_lower.wait_send()

    wait_send(drecv.at[pl.ds(0, nsub - 1)], 10)
    st_iface.wait()
    st_inter.wait()


def shards(
    resid_iface,
    resid_inner,
    weights,
    nbr,
    own2,
    cidx,
    neumann,
    dirichlet,
    coupling,
    coarse_basis,
    group_basis,
    group_inverse,
    top_inverse,
):
    ngroup = lax.axis_size("group")
    nsub = lax.axis_size("sub")
    rows, width = resid_iface.shape[1:]
    inner_width = resid_inner.shape[2]
    group_width = group_inverse.shape[0]
    slots = nsub + 2
    ins = (
        resid_iface[0],
        resid_inner[0],
        weights,
        nbr,
        own2,
        cidx,
        neumann[0],
        dirichlet[0],
        coupling[0],
        coarse_basis[0],
        group_basis,
        group_inverse.T,
        top_inverse,
    )
    v, s = pltpu.VMEM, pltpu.SMEM
    staged = [
        (v if i not in (3, 5) else s)(a.shape, a.dtype) for i, a in enumerate(ins) if i != 4
    ]
    work = [
        v((slots, 1, 128), F32),
        v((rows, width), BF16),
        v((nsub, rows, 128), BF16),
        v((nsub, 1, 128), jnp.int32),
        v((NZ, 32, 128), BF16),
        v((nsub, 32, 128), BF16),
        v((group_width, 128), BF16),
        v((256, 128 * nsub), BF16),
        v((nsub, 128, 128), BF16),
        v((128, 128 * nsub), BF16),
        v((rows, group_width), BF16),
        v((group_width, 128), BF16),
        v((128, group_width), BF16),
        v((128, 128 * NZ), BF16),
        v((ngroup, rows, 128), BF16),
        v((NZ, rows, 128), BF16),
        v((nsub, rows, 128), BF16),
        v((slots, rows, 128), F32),
        v((slots, rows, 128), F32),
        v((nsub, rows, 128), BF16),
        v((nsub, rows, 128), BF16),
        v((2, rows, 128), F32),
        v((slots, rows, 128), BF16),
        v((rows, width), F32),
        v((rows, inner_width), F32),
    ]
    sems = [
        pltpu.SemaphoreType.DMA((13,)),
        pltpu.SemaphoreType.DMA((2,)),
        pltpu.SemaphoreType.DMA((11,)),
        pltpu.SemaphoreType.DMA((11,)),
    ]
    anywhere = pl.BlockSpec(memory_space=pl.ANY)
    iface, inter = pl.pallas_call(
        functools.partial(kernel, ngroup, nsub),
        out_shape=(
            jax.ShapeDtypeStruct((rows, width), F32),
            jax.ShapeDtypeStruct((rows, inner_width), F32),
        ),
        in_specs=[anywhere] * len(ins),
        out_specs=(anywhere, anywhere),
        scratch_shapes=staged + work + sems,
        compiler_params=pltpu.CompilerParams(
            collective_id=0, has_side_effects=True, vmem_limit_bytes=56 * 2**20
        ),
        name="bddc",
    )(*ins)
    return iface[None], inter[None]


def solution(mesh):
    one = P(("group", "sub"), None)
    two = P(("group", "sub"), None, None)
    three = P(("group", "sub"), None, None, None)
    return jax.shard_map(
        shards,
        mesh=mesh,
        in_specs=(two, two, one, one, one, one, three, three, three, two, one, P("group", "sub"), P()),
        out_specs=(two, two),
        check_vma=False,
    )
```

```python
import functools

import jax
import jax.numpy as jnp
from jax import lax
from jax.experimental import pallas as pl
from jax.experimental.pallas import tpu as pltpu
from jax.sharding import PartitionSpec as P

F32 = jnp.float32
BF16 = jnp.bfloat16
MESH = pl.DeviceIdType.MESH
NT = (((1,), (1,)), ((), ()))

NY, NZ = 4, 8


def dot(a, b):
    return jnp.dot(a, b, preferred_element_type=F32)


def dot_nt(a, b):
    return lax.dot_general(a, b, NT, preferred_element_type=F32)


def kernel(
    ngroup,
    nsub,
    resid_h,
    inner_h,
    weights_h,
    nbr_h,
    own_h,
    cidx_h,
    neumann_h,
    dirichlet_h,
    coupling_h,
    cb_h,
    basis_h,
    ginv_h,
    top_h,
    iface,
    inter,
    resid,
    inner,
    weights,
    nbr,
    cidx,
    neumann,
    dirichlet,
    coupling,
    cb,
    basis,
    ginv,
    top,
    scale,
    weighted,
    loc_all,
    own_all,
    bsend,
    bpk,
    bfull,
    ohl,
    hmask,
    lhs,
    lev,
    ohv,
    ginv_pad,
    nsend,
    npk,
    nz,
    p2,
    p3,
    c2,
    nsc,
    scaled,
    dsend,
    drecv,
    face,
    picked,
    quick,
    in_sem,
    send_sem,
    recv_sem,
):
    g = lax.axis_index("group")
    sub = lax.axis_index("sub")
    y, z = sub // NZ, sub % NZ
    par = sub % 2
    slots = nsub + 2
    kn = neumann.shape[0]
    ki = dirichlet.shape[0]
    bi = dirichlet.shape[1]

    loads = [
        (nbr_h, nbr),
        (weights_h, weights),
        (resid_h, resid),
        (cb_h, cb),
        (own_h, own_all.at[sub]),
        (basis_h, basis),
        (neumann_h, neumann),
        (top_h, top),
        (ginv_h, ginv),
        (cidx_h, cidx),
        (inner_h, inner),
        (coupling_h, coupling),
        (dirichlet_h, dirichlet),
    ]
    loads = [pltpu.make_async_copy(s, d, in_sem.at[i]) for i, (s, d) in enumerate(loads)]
    (ld_nbr, ld_w, ld_resid, ld_cb, ld_own, ld_basis, ld_neu, ld_top, ld_ginv, ld_cidx, ld_inner, ld_coup, ld_dir) = loads
    for ld in (ld_nbr, ld_w, ld_resid, ld_cb, ld_basis, ld_own):
        ld.start()

    barrier = pltpu.get_barrier_semaphore()

    def greet_sub(o, _):
        pl.semaphore_signal(barrier, inc=1, device_id=(g, (sub + o) % nsub), device_id_type=MESH)
        return 0

    def greet_group(o, _):
        pl.semaphore_signal(barrier, inc=1, device_id=((g + o) % ngroup, sub), device_id_type=MESH)
        return 0

    lax.fori_loop(1, nsub, greet_sub, 0)
    lax.fori_loop(1, ngroup, greet_group, 0)

    def rcopy(src, dst, phase, tg, ts):
        return pltpu.make_async_remote_copy(
            src_ref=src,
            dst_ref=dst,
            send_sem=send_sem.at[phase],
            recv_sem=recv_sem.at[phase],
            device_id=(tg, ts),
            device_id_type=MESH,
        )

    def wait_recv(ref, phase):
        pltpu.make_async_copy(ref, ref, recv_sem.at[phase]).wait()

    def wait_send(ref, phase):
        pltpu.make_async_copy(ref, ref, send_sem.at[phase]).wait()

    def far_first(i, n):
        return n // 2 + jnp.where(i % 2 == 1, -((i + 1) // 2), i // 2)

    lane = lax.broadcasted_iota(jnp.int32, (1, 128), 1)
    low = lane < 64
    def pack_z(src, dst):
        for k in range(NZ):
            t = slice(128 * (k // 2), 128 * (k // 2) + 128)
            a, b = src[:32, t], src[32:, t]
            if k % 2 == 0:
                pk = jnp.where(low, a, pltpu.roll(b, 64, 1))
            else:
                pk = jnp.where(low, pltpu.roll(a, 64, 1), b)
            dst[k] = pk.astype(BF16)

    def unpack(src, dst, q):
        p = src[q].astype(F32)
        at = q * 64 if isinstance(q, int) else pl.multiple_of(q * 64, 64)
        dst[pl.ds(at, 32), :] = jnp.where(low, p, 0.0).astype(BF16)
        dst[pl.ds(at + 32, 32), :] = jnp.where(low, pltpu.roll(p, 64, 1), 0.0).astype(BF16)

    ld_basis.wait()
    pack_z(basis[...], bsend)
    bpk[sub] = bsend[z]
    ld_own.wait()

    pl.semaphore_wait(barrier, nsub - 1 + ngroup - 1)

    def send_z(i, _):
        tz = (z + far_first(i, NZ)) % NZ
        rcopy(own_all.at[sub], own_all.at[sub], 1, g, y * NZ + tz).start()
        rcopy(bsend.at[tz], bpk.at[sub], 2, g, y * NZ + tz).start()
        return 0

    lax.fori_loop(0, NZ - 1, send_z, 0)

    ld_nbr.wait()
    ld_w.wait()
    ld_resid.wait()
    for j in range(slots):
        sl = pl.ds(128 * j, 128)
        sc = weights[:, sl]
        if j < nsub:
            sc = sc * nbr[0, j].astype(F32)
        scale[j] = sc
        weighted[:, sl] = (sc * resid[:, sl]).astype(BF16)
    ld_cb.wait()
    loc_all[sub] = dot(weighted[...], cb[...]).astype(BF16)

    def send_loc(o, _):
        ts = ((y + far_first(o % NY, NY)) % NY) * NZ + (z + far_first(o // NY, NZ)) % NZ
        rcopy(loc_all.at[sub], loc_all.at[sub], 0, g, ts).start()
        return 0

    lax.fori_loop(0, nsub - 1, send_loc, 0)
    for ld in (ld_top, ld_ginv, ld_coup, ld_dir, ld_inner, ld_neu, ld_cidx):
        ld.start()

    ld_top.wait()
    pack_z(dot(basis[...].astype(BF16), top[...].astype(BF16)), nsend)
    npk[z] = nsend[z]

    def send_n(i, _):
        tz = (z + far_first(i, NZ)) % NZ
        rcopy(nsend.at[tz], npk.at[z], 11, g, y * NZ + tz).start()
        return 0

    lax.fori_loop(0, NZ - 1, send_n, 0)
    mine_rows = pl.ds(pl.multiple_of(par * 64, 64), 64)
    other_rows = pl.ds(pl.multiple_of((1 - par) * 64, 64), 64)
    ld_ginv.wait()
    ginv_pad[mine_rows, :] = ginv[...].astype(BF16)
    ginv_pad[other_rows, :] = jnp.zeros((64, ginv.shape[1]), BF16)

    rows = pl.ds(pl.multiple_of(y * NZ, NZ), NZ)
    wait_recv(own_all.at[pl.ds(0, NZ - 1)], 1)

    def send_own_y(i, _):
        ts = ((y + far_first(i, NY)) % NY) * NZ + z
        rcopy(own_all.at[rows], own_all.at[rows], 3, g, ts).start()
        return 0

    lax.fori_loop(0, NY - 1, send_own_y, 0)
    wait_recv(bpk.at[pl.ds(0, NZ - 1)], 2)

    def send_basis_y(i, _):
        ts = ((y + far_first(i, NY)) % NY) * NZ + z
        rcopy(bpk.at[rows], bpk.at[rows], 4, g, ts).start()
        return 0

    lax.fori_loop(0, NY - 1, send_basis_y, 0)

    ld_coup.wait()
    ld_dir.wait()
    ld_inner.wait()
    for k in range(ki):
        sl = pl.ds(bi * k, bi)
        quick[k] = dot(coupling[k], dirichlet[k]).astype(BF16)
        inter[:, sl] = dot(inner[:, sl].astype(BF16), dirichlet[k])

    wait_recv(own_all.at[pl.ds(0, nsub - NZ)], 3)

    def masks(s, _):
        o = own_all[s]
        lo, hi = o & 255, o >> 8
        ohl[:, pl.ds(pl.multiple_of(s * 128, 128), 128)] = (
            (lax.broadcasted_iota(jnp.int32, (256, 128), 0) == lo).astype(F32).astype(BF16)
        )
        for h in range(8):
            m = (hi == h).astype(F32)
            hmask[s, pl.ds(16 * h, 16), :] = jnp.broadcast_to(m, (16, 128)).astype(BF16)
        return 0

    lax.fori_loop(0, nsub, masks, 0)

    wait_recv(bpk.at[pl.ds(0, nsub - NZ)], 4)

    def unpack_basis(q, _):
        unpack(bpk, bfull, q)
        return 0

    lax.fori_loop(0, nsub, unpack_basis, 0)

    wait_recv(loc_all.at[pl.ds(0, nsub - 1)], 0)
    for s in range(nsub):
        v = loc_all[s]
        for h in range(8):
            lhs[pl.ds(16 * h, 16), pl.ds(128 * s, 128)] = v * hmask[s, pl.ds(16 * h, 16), :]
    level2 = dot_nt(lhs[...], ohl[...])
    for h in range(8):
        lev[:, pl.ds(256 * h, 256)] = level2[16 * h : 16 * h + 16, :].astype(BF16)
    p2[g] = dot(lev[...], bfull[...]).astype(BF16)

    def send_group(o, _):
        rcopy(p2.at[g], p2.at[g], 5, (g + o) % ngroup, sub).start()
        return 0

    lax.fori_loop(1, ngroup, send_group, 0)
    solved = dot_nt(lev[...], ginv_pad[...])
    wait_recv(npk.at[pl.ds(0, NZ - 1)], 11)
    for k in range(NZ):
        unpack(npk, nz, k)
    wait_recv(p2.at[pl.ds(0, ngroup - 1)], 5)
    level3 = p2[0].astype(F32)
    for k in range(1, ngroup):
        level3 = level3 + p2[k].astype(F32)

    part = dot_nt(level3.astype(BF16), nz[...])
    for t in range(NZ // 2):
        own_part = jnp.where(z // 2 == t, solved, 0.0)
        p3[z, pl.ds(16 * t, 16), :] = (part[:, 128 * t : 128 * t + 128] + own_part).astype(BF16)

    def send_part(i, _):
        rcopy(p3.at[z], p3.at[z], 6, g, y * NZ + (z + far_first(i, NZ)) % NZ).start()
        return 0

    lax.fori_loop(0, NZ - 1, send_part, 0)

    def pick(t, _):
        at = pl.multiple_of(t * 256, 256)
        ohv[pl.ds(at, 256), :] = (
            (lax.broadcasted_iota(jnp.int32, (256, 128), 0) + at == own_all[sub]).astype(F32).astype(BF16)
        )
        return 0

    lax.fori_loop(0, 8, pick, 0)
    ld_neu.wait()
    for k in range(kn):
        v = dot(weighted[:, 256 * k : 256 * k + 256], neumann[k])
        nsc[2 * k] = v[:, :128] * scale[2 * k]
        nsc[2 * k + 1] = v[:, 128:] * scale[2 * k + 1]
    wait_recv(p3.at[pl.ds(0, NZ - 1)], 6)
    c2y = p3[0].astype(F32)
    for k in range(1, NZ):
        c2y = c2y + p3[k].astype(F32)
    c2[y] = c2y.astype(BF16)

    def send_coarse(i, _):
        rcopy(c2.at[y], c2.at[y], 7, g, ((y + far_first(i, NY)) % NY) * NZ + z).start()
        return 0

    lax.fori_loop(0, NY - 1, send_coarse, 0)
    wait_recv(c2.at[pl.ds(0, NY - 1)], 7)
    coarse2 = jnp.concatenate(
        [c2[k, 16 * t : 16 * t + 16, :] for k in range(NY) for t in range(NZ // 2)], axis=1
    )
    values = dot(coarse2, ohv[...]).astype(BF16)

    spread = dot_nt(values, cb[pl.ds(128 * nsub, 256), :])
    for i in range(2):
        scaled[nsub + i] = nsc[nsub + i] + scale[nsub + i] * spread[:, 128 * i : 128 * i + 128]

    to_upper = rcopy(scaled.at[nsub + 1], face.at[0], 8, jnp.minimum(g + 1, ngroup - 1), sub)
    to_lower = rcopy(scaled.at[nsub], face.at[1], 9, jnp.maximum(g - 1, 0), sub)

    @pl.when(g < ngroup - 1)
    def _():
        to_upper.start()

    @pl.when(g > 0)
    def _():
        to_lower.start()

    for c in range(NY):
        ty = (y + (2, 1, 3, 0)[c]) % NY
        first = ty * NZ
        spread = dot_nt(values, cb[pl.ds(pl.multiple_of(first * 128, 1024), 1024), :])
        for i in range(NZ):
            v = nsc[first + i] + scale[first + i] * spread[:, 128 * i : 128 * i + 128]
            scaled[first + i] = v
            dsend[first + i] = v.astype(BF16)

        def send_slot(o, _):
            to = first + (z + far_first(o, NZ)) % NZ
            rcopy(dsend.at[to], drecv.at[sub], 10, g, to).start()
            return 0

        lax.fori_loop(0, NZ if c < NY - 1 else NZ - 1, send_slot, 0)
    drecv[sub] = dsend[sub]

    @pl.when(g > 0)
    def _():
        to_upper.wait_recv()

    @pl.when(g == 0)
    def _():
        face[0] = jnp.zeros(face.shape[1:], F32)

    @pl.when(g < ngroup - 1)
    def _():
        to_lower.wait_recv()

    @pl.when(g == ngroup - 1)
    def _():
        face[1] = jnp.zeros(face.shape[1:], F32)

    ld_cidx.wait()
    wait_recv(drecv.at[pl.ds(0, nsub - 1)], 10)
    for j in range(slots):
        got = drecv[j].astype(F32) if j < nsub else face[j - nsub]
        v = scaled[j] + got
        iface[:, pl.ds(128 * j, 128)] = v
        picked[j] = v.astype(BF16)
    for k in range(ki):
        at = 2 * cidx[0, k]
        block = jnp.concatenate([picked[at], picked[at + 1]], axis=1)
        sl = pl.ds(bi * k, bi)
        inter[:, sl] = inter[:, sl] - dot(block, quick[k])

    wait_send(loc_all.at[pl.ds(0, nsub - 1)], 0)
    wait_send(own_all.at[pl.ds(0, NZ - 1)], 1)
    wait_send(bpk.at[pl.ds(0, NZ - 1)], 2)
    wait_send(own_all.at[pl.ds(0, nsub - NZ)], 3)
    wait_send(bpk.at[pl.ds(0, nsub - NZ)], 4)
    wait_send(p2.at[pl.ds(0, ngroup - 1)], 5)
    wait_send(p3.at[pl.ds(0, NZ - 1)], 6)
    wait_send(c2.at[pl.ds(0, NY - 1)], 7)
    wait_send(npk.at[pl.ds(0, NZ - 1)], 11)

    @pl.when(g < ngroup - 1)
    def _():
        to_upper.wait_send()

    @pl.when(g > 0)
    def _():
        to_lower.wait_send()

    wait_send(drecv.at[pl.ds(0, nsub - 1)], 10)


def shards(
    resid_iface,
    resid_inner,
    weights,
    nbr,
    own2,
    cidx,
    neumann,
    dirichlet,
    coupling,
    coarse_basis,
    group_basis,
    group_inverse,
    top_inverse,
):
    ngroup = lax.axis_size("group")
    nsub = lax.axis_size("sub")
    rows, width = resid_iface.shape[1:]
    inner_width = resid_inner.shape[2]
    group_width = group_inverse.shape[0]
    slots = nsub + 2
    ins = (
        resid_iface[0],
        resid_inner[0],
        weights,
        nbr,
        own2,
        cidx,
        neumann[0],
        dirichlet[0],
        coupling[0],
        coarse_basis[0],
        group_basis,
        group_inverse.T,
        top_inverse,
    )
    v, s = pltpu.VMEM, pltpu.SMEM
    staged = [
        (v if i not in (3, 5) else s)(a.shape, a.dtype) for i, a in enumerate(ins) if i != 4
    ]
    work = [
        v((slots, 1, 128), F32),
        v((rows, width), BF16),
        v((nsub, rows, 128), BF16),
        v((nsub, 1, 128), jnp.int32),
        v((NZ, 32, 128), BF16),
        v((nsub, 32, 128), BF16),
        v((group_width, 128), BF16),
        v((256, 128 * nsub), BF16),
        v((nsub, 128, 128), BF16),
        v((128, 128 * nsub), BF16),
        v((rows, group_width), BF16),
        v((group_width, 128), BF16),
        v((128, group_width), BF16),
        v((NZ, 32, 128), BF16),
        v((NZ, 32, 128), BF16),
        v((64 * NZ, 128), BF16),
        v((ngroup, rows, 128), BF16),
        v((NZ, rows * NZ // 2, 128), BF16),
        v((NY, rows * NZ // 2, 128), BF16),
        v((slots, rows, 128), F32),
        v((slots, rows, 128), F32),
        v((nsub, rows, 128), BF16),
        v((nsub, rows, 128), BF16),
        v((2, rows, 128), F32),
        v((slots, rows, 128), BF16),
        v(coupling.shape[1:], BF16),
    ]
    sems = [
        pltpu.SemaphoreType.DMA((13,)),
        pltpu.SemaphoreType.DMA((12,)),
        pltpu.SemaphoreType.DMA((12,)),
    ]
    anywhere = pl.BlockSpec(memory_space=pl.ANY)
    iface, inter = pl.pallas_call(
        functools.partial(kernel, ngroup, nsub),
        out_shape=(
            pltpu.VMEM((rows, width), F32),
            pltpu.VMEM((rows, inner_width), F32),
        ),
        in_specs=[anywhere] * len(ins),
        out_specs=(pl.BlockSpec(memory_space=pltpu.VMEM),) * 2,
        scratch_shapes=staged + work + sems,
        compiler_params=pltpu.CompilerParams(
            collective_id=0, has_side_effects=True, vmem_limit_bytes=60 * 2**20
        ),
        name="bddc",
    )(*ins)
    return iface[None], inter[None]


def solution(mesh):
    one = P(("group", "sub"), None)
    two = P(("group", "sub"), None, None)
    three = P(("group", "sub"), None, None, None)
    return jax.shard_map(
        shards,
        mesh=mesh,
        in_specs=(two, two, one, one, one, one, three, three, three, two, one, P("group", "sub"), P()),
        out_specs=(two, two),
        check_vma=False,
    )
```

```python
import functools

import jax
import jax.numpy as jnp
from jax import lax
from jax.experimental import pallas as pl
from jax.experimental.pallas import tpu as pltpu
from jax.sharding import PartitionSpec as P

F32 = jnp.float32
BF16 = jnp.bfloat16
MESH = pl.DeviceIdType.MESH
NT = (((1,), (1,)), ((), ()))

NY, NZ = 4, 8


def dot(a, b):
    return jnp.dot(a, b, preferred_element_type=F32)


def dot_nt(a, b):
    return lax.dot_general(a, b, NT, preferred_element_type=F32)


def kernel(
    ngroup,
    nsub,
    resid_h,
    inner_h,
    weights_h,
    nbr_h,
    own_h,
    cidx_h,
    neumann_h,
    dirichlet_h,
    coupling_h,
    cb_h,
    basis_h,
    ginv_h,
    top_h,
    iface,
    inter,
    resid,
    inner,
    weights,
    nbr,
    cidx,
    neumann,
    dirichlet,
    coupling,
    cb,
    basis,
    ginv,
    top,
    scale,
    weighted,
    loc_all,
    own_all,
    bsend,
    bpk,
    bfull,
    ohl,
    lhs,
    lev_send,
    lev_recv,
    lev,
    ohv,
    ginv_pad,
    nsend,
    npk,
    nz,
    p2,
    p3,
    c2,
    nsc,
    scaled,
    dsend,
    drecv,
    face,
    picked,
    quick,
    in_sem,
    send_sem,
    recv_sem,
):
    g = lax.axis_index("group")
    sub = lax.axis_index("sub")
    y, z = sub // NZ, sub % NZ
    par = sub % 2
    slots = nsub + 2
    kn = neumann.shape[0]
    ki = dirichlet.shape[0]
    bi = dirichlet.shape[1]

    loads = [
        (nbr_h, nbr),
        (weights_h, weights),
        (resid_h, resid),
        (cb_h, cb),
        (own_h, own_all.at[z]),
        (basis_h, basis),
        (neumann_h, neumann),
        (top_h, top),
        (ginv_h, ginv),
        (cidx_h, cidx),
        (inner_h, inner),
        (coupling_h, coupling),
        (dirichlet_h, dirichlet),
    ]
    loads = [pltpu.make_async_copy(s, d, in_sem.at[i]) for i, (s, d) in enumerate(loads)]
    (ld_nbr, ld_w, ld_resid, ld_cb, ld_own, ld_basis, ld_neu, ld_top, ld_ginv, ld_cidx, ld_inner, ld_coup, ld_dir) = loads
    for ld in (ld_cb, ld_resid, ld_nbr, ld_w, ld_basis, ld_own):
        ld.start()

    def far_first(i, n):
        return n // 2 + jnp.where(i % 2 == 1, -((i + 1) // 2), i // 2)

    def z_at(i):
        return (z + far_first(i, NZ)) % NZ

    def y_at(i):
        return (y + far_first(i, NY)) % NY

    def plane_peer(o):
        tg = (g // 2 + far_first(o // (2 * NY), ngroup // 2)) % (ngroup // 2) * 2 + (g + 1 - o % 2) % 2
        return tg, y_at(o // 2 % NY) * NZ + z

    barrier = pltpu.get_barrier_semaphore()
    plane = ngroup * NY

    def greet_z(i, _):
        pl.semaphore_signal(barrier, inc=1, device_id=(g, y * NZ + z_at(i)), device_id_type=MESH)
        return 0

    def greet_plane(o, _):
        pl.semaphore_signal(barrier, inc=1, device_id=plane_peer(o), device_id_type=MESH)
        return 0

    lax.fori_loop(0, NZ - 1, greet_z, 0)
    lax.fori_loop(0, plane - 1, greet_plane, 0)

    def rcopy(src, dst, phase, tg, ts):
        return pltpu.make_async_remote_copy(
            src_ref=src,
            dst_ref=dst,
            send_sem=send_sem.at[phase],
            recv_sem=recv_sem.at[phase],
            device_id=(tg, ts),
            device_id_type=MESH,
        )

    def wait_recv(ref, phase):
        pltpu.make_async_copy(ref, ref, recv_sem.at[phase]).wait()

    def wait_send(ref, phase):
        pltpu.make_async_copy(ref, ref, send_sem.at[phase]).wait()

    lane = lax.broadcasted_iota(jnp.int32, (1, 128), 1)
    low = lane < 64
    def pack_z(src, dst):
        for k in range(NZ):
            t = slice(128 * (k // 2), 128 * (k // 2) + 128)
            a, b = src[:32, t], src[32:, t]
            if k % 2 == 0:
                pk = jnp.where(low, a, pltpu.roll(b, 64, 1))
            else:
                pk = jnp.where(low, pltpu.roll(a, 64, 1), b)
            dst[k] = pk.astype(BF16)

    def unpack(src, dst, q):
        p = src[q].astype(F32)
        at = q * 64 if isinstance(q, int) else pl.multiple_of(q * 64, 64)
        dst[pl.ds(at, 32), :] = jnp.where(low, p, 0.0).astype(BF16)
        dst[pl.ds(at + 32, 32), :] = jnp.where(low, pltpu.roll(p, 64, 1), 0.0).astype(BF16)

    ld_nbr.wait()
    ld_w.wait()
    ld_resid.wait()
    for j in range(slots):
        sl = pl.ds(128 * j, 128)
        sc = weights[:, sl]
        if j < nsub:
            sc = sc * nbr[0, j].astype(F32)
        scale[j] = sc
        weighted[:, sl] = (sc * resid[:, sl]).astype(BF16)
    ld_cb.wait()
    loc_all[z] = dot(weighted[...], cb[...]).astype(BF16)
    ld_basis.wait()
    pack_z(basis[...], bsend)
    bpk[z] = bsend[z]
    ld_own.wait()

    for ld in (ld_top, ld_ginv, ld_neu, ld_coup, ld_dir, ld_inner, ld_cidx):
        ld.start()

    pl.semaphore_wait(barrier, NZ - 1 + plane - 1)

    def send_loc(i, _):
        tz = z_at(i)
        rcopy(own_all.at[z], own_all.at[z], 1, g, y * NZ + tz).start()
        rcopy(loc_all.at[z], loc_all.at[z], 0, g, y * NZ + tz).start()
        return 0

    lax.fori_loop(0, NZ - 1, send_loc, 0)

    def send_z(i, _):
        tz = z_at(i)
        rcopy(bsend.at[tz], bpk.at[z], 2, g, y * NZ + tz).start()
        return 0

    lax.fori_loop(0, NZ - 1, send_z, 0)

    ld_top.wait()
    pack_z(dot(basis[...].astype(BF16), top[...].astype(BF16)), nsend)
    npk[z] = nsend[z]
    mine_rows = pl.ds(pl.multiple_of(par * 64, 64), 64)
    other_rows = pl.ds(pl.multiple_of((1 - par) * 64, 64), 64)
    ld_ginv.wait()
    ginv_pad[mine_rows, :] = ginv[...].astype(BF16)
    ginv_pad[other_rows, :] = jnp.zeros((64, ginv.shape[1]), BF16)

    wait_recv(own_all.at[pl.ds(0, NZ - 1)], 1)
    wait_recv(loc_all.at[pl.ds(0, NZ - 1)], 0)
    count = lax.broadcasted_iota(jnp.int32, (256, 128), 0).astype(F32).astype(BF16)
    one, nil = jnp.ones((256, 128), BF16), jnp.zeros((256, 128), BF16)
    for s in range(NZ):
        at = pl.ds(128 * s, 128)
        o = own_all[s]
        lo = (o & 255).astype(F32).astype(BF16)
        hi = (o >> 8).astype(F32).astype(BF16)
        ohl[:, at] = jnp.where(count == lo, one, nil)
        v = loc_all[s]
        for h in range(8):
            lhs[pl.ds(16 * h, 16), at] = jnp.where(hi == h, v, nil[:16])
    level2 = dot_nt(lhs[...], ohl[...])
    for h in range(8):
        lev_send[h // 2, :, pl.ds(256 * (h % 2), 256)] = level2[16 * h : 16 * h + 16, :].astype(BF16)

    def send_lev(i, _):
        ty = y_at(i)
        rcopy(lev_send.at[ty], lev_recv.at[y], 4, g, ty * NZ + z).start()
        return 0

    lax.fori_loop(0, NY - 1, send_lev, 0)
    lev_recv[y] = lev_send[y]
    wait_recv(bpk.at[pl.ds(0, NZ - 1)], 2)
    for k in range(NZ):
        unpack(bpk, bfull, k)
    wait_recv(lev_recv.at[pl.ds(0, NY - 1)], 4)
    mine = lev_recv[0].astype(F32)
    for k in range(1, NY):
        mine = mine + lev_recv[k].astype(F32)
    lev[y] = mine.astype(BF16)
    p2[g * NY + y] = dot(lev[y], bfull[...]).astype(BF16)

    def send_plane(o, _):
        tg, ts = plane_peer(o)
        rcopy(p2.at[g * NY + y], p2.at[g * NY + y], 5, tg, ts).start()
        return 0

    lax.fori_loop(0, plane - 1, send_plane, 0)

    def send_level2(i, _):
        rcopy(lev.at[y], lev.at[y], 3, g, y_at(i) * NZ + z).start()
        return 0

    lax.fori_loop(0, NY - 1, send_level2, 0)

    def send_n(i, _):
        tz = z_at(i)
        rcopy(nsend.at[tz], npk.at[z], 11, g, y * NZ + tz).start()
        return 0

    lax.fori_loop(0, NZ - 1, send_n, 0)
    ld_coup.wait()
    ld_dir.wait()
    ld_inner.wait()
    for k in range(ki):
        sl = pl.ds(bi * k, bi)
        quick[k] = dot(coupling[k], dirichlet[k]).astype(BF16)
        inter[:, sl] = dot(inner[:, sl].astype(BF16), dirichlet[k])
    wait_recv(lev.at[pl.ds(0, NY - 1)], 3)
    solved = dot_nt(jnp.concatenate([lev[k] for k in range(NY)], axis=1), ginv_pad[...])
    wait_recv(npk.at[pl.ds(0, NZ - 1)], 11)
    for k in range(NZ):
        unpack(npk, nz, k)
    wait_recv(p2.at[pl.ds(0, plane - 1)], 5)
    level3 = p2[0].astype(F32)
    for k in range(1, plane):
        level3 = level3 + p2[k].astype(F32)

    part = dot_nt(level3.astype(BF16), nz[...])
    for t in range(NZ // 2):
        own_part = jnp.where(z // 2 == t, solved, 0.0)
        p3[z, pl.ds(16 * t, 16), :] = (part[:, 128 * t : 128 * t + 128] + own_part).astype(BF16)

    def send_part(i, _):
        rcopy(p3.at[z], p3.at[z], 6, g, y * NZ + z_at(i)).start()
        return 0

    lax.fori_loop(0, NZ - 1, send_part, 0)

    def pick(t, _):
        at = pl.multiple_of(t * 256, 256)
        ohv[pl.ds(at, 256), :] = (
            (lax.broadcasted_iota(jnp.int32, (256, 128), 0) + at == own_all[z]).astype(F32).astype(BF16)
        )
        return 0

    lax.fori_loop(0, 8, pick, 0)
    ld_neu.wait()
    for k in range(kn):
        v = dot(weighted[:, 256 * k : 256 * k + 256], neumann[k])
        nsc[2 * k] = v[:, :128] * scale[2 * k]
        nsc[2 * k + 1] = v[:, 128:] * scale[2 * k + 1]
    wait_recv(p3.at[pl.ds(0, NZ - 1)], 6)
    c2y = p3[0].astype(F32)
    for k in range(1, NZ):
        c2y = c2y + p3[k].astype(F32)
    c2[y] = c2y.astype(BF16)

    def send_coarse(i, _):
        rcopy(c2.at[y], c2.at[y], 7, g, y_at(i) * NZ + z).start()
        return 0

    lax.fori_loop(0, NY - 1, send_coarse, 0)
    wait_recv(c2.at[pl.ds(0, NY - 1)], 7)
    coarse2 = jnp.concatenate(
        [c2[k, 16 * t : 16 * t + 16, :] for k in range(NY) for t in range(NZ // 2)], axis=1
    )
    values = dot(coarse2, ohv[...]).astype(BF16)

    spread = dot_nt(values, cb[pl.ds(128 * nsub, 256), :])
    for i in range(2):
        scaled[nsub + i] = nsc[nsub + i] + scale[nsub + i] * spread[:, 128 * i : 128 * i + 128]

    to_upper = rcopy(scaled.at[nsub + 1], face.at[0], 8, jnp.minimum(g + 1, ngroup - 1), sub)
    to_lower = rcopy(scaled.at[nsub], face.at[1], 9, jnp.maximum(g - 1, 0), sub)

    @pl.when(g < ngroup - 1)
    def _():
        to_upper.start()

    @pl.when(g > 0)
    def _():
        to_lower.start()

    for c in range(NY):
        ty = (y + (2, 1, 3, 0)[c]) % NY
        first = ty * NZ
        spread = dot_nt(values, cb[pl.ds(pl.multiple_of(first * 128, 1024), 1024), :])
        for i in range(NZ):
            v = nsc[first + i] + scale[first + i] * spread[:, 128 * i : 128 * i + 128]
            scaled[first + i] = v
            dsend[first + i] = v.astype(BF16)

        def send_slot(o, _):
            to = first + z_at(o)
            rcopy(dsend.at[to], drecv.at[sub], 10, g, to).start()
            return 0

        lax.fori_loop(0, NZ if c < NY - 1 else NZ - 1, send_slot, 0)
    drecv[sub] = dsend[sub]

    @pl.when(g > 0)
    def _():
        to_upper.wait_recv()

    @pl.when(g == 0)
    def _():
        face[0] = jnp.zeros(face.shape[1:], F32)

    @pl.when(g < ngroup - 1)
    def _():
        to_lower.wait_recv()

    @pl.when(g == ngroup - 1)
    def _():
        face[1] = jnp.zeros(face.shape[1:], F32)

    ld_cidx.wait()
    wait_recv(drecv.at[pl.ds(0, nsub - 1)], 10)
    for j in range(slots):
        got = drecv[j].astype(F32) if j < nsub else face[j - nsub]
        v = scaled[j] + got
        iface[:, pl.ds(128 * j, 128)] = v
        picked[j] = v.astype(BF16)
    for k in range(ki):
        at = 2 * cidx[0, k]
        block = jnp.concatenate([picked[at], picked[at + 1]], axis=1)
        sl = pl.ds(bi * k, bi)
        inter[:, sl] = inter[:, sl] - dot(block, quick[k])

    wait_send(loc_all.at[pl.ds(0, NZ - 1)], 0)
    wait_send(own_all.at[pl.ds(0, NZ - 1)], 1)
    wait_send(lev.at[pl.ds(0, NY - 1)], 3)
    wait_send(lev_recv.at[pl.ds(0, NY - 1)], 4)
    wait_send(bpk.at[pl.ds(0, NZ - 1)], 2)
    wait_send(p2.at[pl.ds(0, plane - 1)], 5)
    wait_send(p3.at[pl.ds(0, NZ - 1)], 6)
    wait_send(c2.at[pl.ds(0, NY - 1)], 7)
    wait_send(npk.at[pl.ds(0, NZ - 1)], 11)

    @pl.when(g < ngroup - 1)
    def _():
        to_upper.wait_send()

    @pl.when(g > 0)
    def _():
        to_lower.wait_send()

    wait_send(drecv.at[pl.ds(0, nsub - 1)], 10)


def shards(
    resid_iface,
    resid_inner,
    weights,
    nbr,
    own2,
    cidx,
    neumann,
    dirichlet,
    coupling,
    coarse_basis,
    group_basis,
    group_inverse,
    top_inverse,
):
    ngroup = lax.axis_size("group")
    nsub = lax.axis_size("sub")
    rows, width = resid_iface.shape[1:]
    inner_width = resid_inner.shape[2]
    group_width = group_inverse.shape[0]
    slots = nsub + 2
    ins = (
        resid_iface[0],
        resid_inner[0],
        weights,
        nbr,
        own2,
        cidx,
        neumann[0],
        dirichlet[0],
        coupling[0],
        coarse_basis[0],
        group_basis,
        group_inverse.T,
        top_inverse,
    )
    v, s = pltpu.VMEM, pltpu.SMEM
    staged = [
        (v if i not in (3, 5) else s)(a.shape, a.dtype) for i, a in enumerate(ins) if i != 4
    ]
    work = [
        v((slots, 1, 128), F32),
        v((rows, width), BF16),
        v((NZ, rows, 128), BF16),
        v((NZ, 1, 128), jnp.int32),
        v((NZ, 32, 128), BF16),
        v((NZ, 32, 128), BF16),
        v((64 * NZ, 128), BF16),
        v((256, 128 * NZ), BF16),
        v((128, 128 * NZ), BF16),
        v((NY, rows, group_width // NY), BF16),
        v((NY, rows, group_width // NY), BF16),
        v((NY, rows, group_width // NY), BF16),
        v((group_width, 128), BF16),
        v((128, group_width), BF16),
        v((NZ, 32, 128), BF16),
        v((NZ, 32, 128), BF16),
        v((64 * NZ, 128), BF16),
        v((ngroup * NY, rows, 128), BF16),
        v((NZ, rows * NZ // 2, 128), BF16),
        v((NY, rows * NZ // 2, 128), BF16),
        v((slots, rows, 128), F32),
        v((slots, rows, 128), F32),
        v((nsub, rows, 128), BF16),
        v((nsub, rows, 128), BF16),
        v((2, rows, 128), F32),
        v((slots, rows, 128), BF16),
        v(coupling.shape[1:], BF16),
    ]
    sems = [
        pltpu.SemaphoreType.DMA((13,)),
        pltpu.SemaphoreType.DMA((12,)),
        pltpu.SemaphoreType.DMA((12,)),
    ]
    anywhere = pl.BlockSpec(memory_space=pl.ANY)
    iface, inter = pl.pallas_call(
        functools.partial(kernel, ngroup, nsub),
        out_shape=(
            pltpu.VMEM((rows, width), F32),
            pltpu.VMEM((rows, inner_width), F32),
        ),
        in_specs=[anywhere] * len(ins),
        out_specs=(pl.BlockSpec(memory_space=pltpu.VMEM),) * 2,
        scratch_shapes=staged + work + sems,
        compiler_params=pltpu.CompilerParams(
            collective_id=0, has_side_effects=True, vmem_limit_bytes=60 * 2**20
        ),
        name="bddc",
    )(*ins)
    return iface[None], inter[None]


def solution(mesh):
    one = P(("group", "sub"), None)
    two = P(("group", "sub"), None, None)
    three = P(("group", "sub"), None, None, None)
    return jax.shard_map(
        shards,
        mesh=mesh,
        in_specs=(two, two, one, one, one, one, three, three, three, two, one, P("group", "sub"), P()),
        out_specs=(two, two),
        check_vma=False,
    )
```

```python
import functools

import jax
import jax.numpy as jnp
from jax import lax
from jax.experimental import pallas as pl
from jax.experimental.pallas import tpu as pltpu
from jax.sharding import PartitionSpec as P

F32 = jnp.float32
BF16 = jnp.bfloat16
MESH = pl.DeviceIdType.MESH
NT = (((1,), (1,)), ((), ()))

NY, NZ = 4, 8


def dot(a, b):
    return jnp.dot(a, b, preferred_element_type=F32)


def dot_nt(a, b):
    return lax.dot_general(a, b, NT, preferred_element_type=F32)


def kernel(
    ngroup,
    nsub,
    resid_h,
    inner_h,
    weights_h,
    nbr_h,
    own_h,
    cidx_h,
    neumann_h,
    dirichlet_h,
    coupling_h,
    cb_h,
    basis_h,
    ginv_h,
    top_h,
    iface,
    inter,
    resid,
    inner,
    weights,
    nbr,
    cidx,
    neumann,
    dirichlet,
    coupling,
    cb,
    basis,
    ginv,
    top,
    scale,
    weighted,
    loc_all,
    own_all,
    bsend,
    bpk,
    bfull,
    ohl,
    lhs,
    lev_send,
    lev_recv,
    lev,
    ohv,
    ginv_pad,
    nsend,
    npk,
    nz,
    p2,
    p3,
    c2,
    nsc,
    scaled,
    dsend,
    drecv,
    face,
    picked,
    quick,
    in_sem,
    send_sem,
    recv_sem,
):
    g = lax.axis_index("group")
    sub = lax.axis_index("sub")
    y, z = sub // NZ, sub % NZ
    par = sub % 2
    slots = nsub + 2
    kn = neumann.shape[0]
    ki = dirichlet.shape[0]
    bi = dirichlet.shape[1]

    loads = [
        (nbr_h, nbr),
        (weights_h, weights),
        (resid_h, resid),
        (cb_h, cb),
        (own_h, own_all.at[z]),
        (basis_h, basis),
        (neumann_h, neumann),
        (top_h, top),
        (ginv_h, ginv),
        (cidx_h, cidx),
        (inner_h, inner),
        (coupling_h, coupling),
        (dirichlet_h, dirichlet),
    ]
    loads = [pltpu.make_async_copy(s, d, in_sem.at[i]) for i, (s, d) in enumerate(loads)]
    (ld_nbr, ld_w, ld_resid, ld_cb, ld_own, ld_basis, ld_neu, ld_top, ld_ginv, ld_cidx, ld_inner, ld_coup, ld_dir) = loads

    def far_first(i, n):
        return n // 2 + jnp.where(i % 2 == 1, -((i + 1) // 2), i // 2)

    def z_at(i):
        return (z + far_first(i, NZ)) % NZ

    def y_at(i):
        return (y + far_first(i, NY)) % NY

    def plane_peer(o):
        tg = (g // 2 + far_first(o // (2 * NY), ngroup // 2)) % (ngroup // 2) * 2 + (g + 1 - o % 2) % 2
        return tg, y_at(o // 2 % NY) * NZ + z

    barrier = pltpu.get_barrier_semaphore()
    plane = ngroup * NY

    def greet_z(i, _):
        pl.semaphore_signal(barrier, inc=1, device_id=(g, y * NZ + z_at(i)), device_id_type=MESH)
        return 0

    def greet_plane(o, _):
        pl.semaphore_signal(barrier, inc=1, device_id=plane_peer(o), device_id_type=MESH)
        return 0

    lax.fori_loop(0, NZ - 1, greet_z, 0)
    for ld in (ld_cb, ld_resid, ld_nbr, ld_w, ld_basis, ld_own):
        ld.start()
    lax.fori_loop(0, plane - 1, greet_plane, 0)

    def rcopy(src, dst, phase, tg, ts):
        return pltpu.make_async_remote_copy(
            src_ref=src,
            dst_ref=dst,
            send_sem=send_sem.at[phase],
            recv_sem=recv_sem.at[phase],
            device_id=(tg, ts),
            device_id_type=MESH,
        )

    def wait_recv(ref, phase):
        pltpu.make_async_copy(ref, ref, recv_sem.at[phase]).wait()

    def wait_send(ref, phase):
        pltpu.make_async_copy(ref, ref, send_sem.at[phase]).wait()

    lane = lax.broadcasted_iota(jnp.int32, (1, 128), 1)
    low = lane < 64
    def pack_z(src, dst):
        for k in range(NZ):
            t = slice(128 * (k // 2), 128 * (k // 2) + 128)
            a, b = src[:32, t], src[32:, t]
            if k % 2 == 0:
                pk = jnp.where(low, a, pltpu.roll(b, 64, 1))
            else:
                pk = jnp.where(low, pltpu.roll(a, 64, 1), b)
            dst[k] = pk.astype(BF16)

    def unpack(src, dst, q):
        p = src[q].astype(F32)
        at = q * 64 if isinstance(q, int) else pl.multiple_of(q * 64, 64)
        dst[pl.ds(at, 32), :] = jnp.where(low, p, 0.0).astype(BF16)
        dst[pl.ds(at + 32, 32), :] = jnp.where(low, pltpu.roll(p, 64, 1), 0.0).astype(BF16)

    ld_nbr.wait()
    ld_w.wait()
    ld_resid.wait()
    for j in range(slots):
        sl = pl.ds(128 * j, 128)
        sc = weights[:, sl]
        if j < nsub:
            sc = sc * nbr[0, j].astype(F32)
        scale[j] = sc
        weighted[:, sl] = (sc * resid[:, sl]).astype(BF16)
    ld_cb.wait()
    loc_all[z] = dot(weighted[...], cb[...]).astype(BF16)
    ld_basis.wait()
    pack_z(basis[...], bsend)
    bpk[z] = bsend[z]
    ld_own.wait()

    for ld in (ld_top, ld_ginv, ld_neu, ld_coup, ld_dir, ld_inner, ld_cidx):
        ld.start()

    pl.semaphore_wait(barrier, NZ - 1 + plane - 1)

    def send_loc(i, _):
        tz = z_at(i)
        rcopy(own_all.at[z], own_all.at[z], 1, g, y * NZ + tz).start()
        rcopy(loc_all.at[z], loc_all.at[z], 0, g, y * NZ + tz).start()
        return 0

    lax.fori_loop(0, NZ - 1, send_loc, 0)

    def send_z(i, _):
        tz = z_at(i)
        rcopy(bsend.at[tz], bpk.at[z], 2, g, y * NZ + tz).start()
        return 0

    lax.fori_loop(0, NZ - 1, send_z, 0)

    ld_top.wait()
    pack_z(dot(basis[...].astype(BF16), top[...].astype(BF16)), nsend)
    npk[z] = nsend[z]

    def send_n(i, _):
        tz = z_at(i)
        rcopy(nsend.at[tz], npk.at[z], 11, g, y * NZ + tz).start()
        return 0

    lax.fori_loop(0, NZ - 1, send_n, 0)
    mine_rows = pl.ds(pl.multiple_of(par * 64, 64), 64)
    other_rows = pl.ds(pl.multiple_of((1 - par) * 64, 64), 64)
    ld_ginv.wait()
    ginv_pad[mine_rows, :] = ginv[...].astype(BF16)
    ginv_pad[other_rows, :] = jnp.zeros((64, ginv.shape[1]), BF16)

    wait_recv(own_all.at[pl.ds(0, NZ - 1)], 1)
    wait_recv(loc_all.at[pl.ds(0, NZ - 1)], 0)
    count = lax.broadcasted_iota(jnp.int32, (256, 128), 0).astype(F32).astype(BF16)
    one, nil = jnp.ones((256, 128), BF16), jnp.zeros((256, 128), BF16)
    for s in range(NZ):
        at = pl.ds(128 * s, 128)
        o = own_all[s]
        lo = (o & 255).astype(F32).astype(BF16)
        hi = (o >> 8).astype(F32).astype(BF16)
        ohl[:, at] = jnp.where(count == lo, one, nil)
        v = loc_all[s]
        for h in range(8):
            lhs[pl.ds(16 * h, 16), at] = jnp.where(hi == h, v, nil[:16])
    level2 = dot_nt(lhs[...], ohl[...])
    for h in range(8):
        lev_send[h // 2, :, pl.ds(256 * (h % 2), 256)] = level2[16 * h : 16 * h + 16, :].astype(BF16)

    def send_lev(i, _):
        ty = y_at(i)
        rcopy(lev_send.at[ty], lev_recv.at[y], 4, g, ty * NZ + z).start()
        return 0

    lax.fori_loop(0, NY - 1, send_lev, 0)
    lev_recv[y] = lev_send[y]

    wait_recv(bpk.at[pl.ds(0, NZ - 1)], 2)
    for k in range(NZ):
        unpack(bpk, bfull, k)
    wait_recv(lev_recv.at[pl.ds(0, NY - 1)], 4)
    mine = lev_recv[0].astype(F32)
    for k in range(1, NY):
        mine = mine + lev_recv[k].astype(F32)
    lev[y] = mine.astype(BF16)
    p2[g * NY + y] = dot(lev[y], bfull[...]).astype(BF16)

    def send_plane(o, _):
        tg, ts = plane_peer(o)
        rcopy(p2.at[g * NY + y], p2.at[g * NY + y], 5, tg, ts).start()
        return 0

    lax.fori_loop(0, plane - 1, send_plane, 0)

    def send_level2(i, _):
        rcopy(lev.at[y], lev.at[y], 3, g, y_at(i) * NZ + z).start()
        return 0

    lax.fori_loop(0, NY - 1, send_level2, 0)

    wait_recv(lev.at[pl.ds(0, NY - 1)], 3)
    solved = dot_nt(jnp.concatenate([lev[k] for k in range(NY)], axis=1), ginv_pad[...])
    wait_recv(npk.at[pl.ds(0, NZ - 1)], 11)
    for k in range(NZ):
        unpack(npk, nz, k)
    wait_recv(p2.at[pl.ds(0, plane - 1)], 5)
    level3 = p2[0].astype(F32)
    for k in range(1, plane):
        level3 = level3 + p2[k].astype(F32)

    part = dot_nt(level3.astype(BF16), nz[...])
    for t in range(NZ // 2):
        own_part = jnp.where(z // 2 == t, solved, 0.0)
        p3[z, pl.ds(16 * t, 16), :] = (part[:, 128 * t : 128 * t + 128] + own_part).astype(BF16)

    def send_part(i, _):
        rcopy(p3.at[z], p3.at[z], 6, g, y * NZ + z_at(i)).start()
        return 0

    lax.fori_loop(0, NZ - 1, send_part, 0)

    def pick(t, _):
        at = pl.multiple_of(t * 256, 256)
        ohv[pl.ds(at, 256), :] = (
            (lax.broadcasted_iota(jnp.int32, (256, 128), 0) + at == own_all[z]).astype(F32).astype(BF16)
        )
        return 0

    lax.fori_loop(0, 8, pick, 0)
    wait_recv(p3.at[pl.ds(0, NZ - 1)], 6)
    c2y = p3[0].astype(F32)
    for k in range(1, NZ):
        c2y = c2y + p3[k].astype(F32)
    c2[y] = c2y.astype(BF16)

    def send_coarse(i, _):
        rcopy(c2.at[y], c2.at[y], 7, g, y_at(i) * NZ + z).start()
        return 0

    lax.fori_loop(0, NY - 1, send_coarse, 0)
    ld_neu.wait()
    for k in range(kn):
        v = dot(weighted[:, 256 * k : 256 * k + 256], neumann[k])
        nsc[2 * k] = v[:, :128] * scale[2 * k]
        nsc[2 * k + 1] = v[:, 128:] * scale[2 * k + 1]
    wait_recv(c2.at[pl.ds(0, NY - 1)], 7)
    coarse2 = jnp.concatenate(
        [c2[k, 16 * t : 16 * t + 16, :] for k in range(NY) for t in range(NZ // 2)], axis=1
    )
    values = dot(coarse2, ohv[...]).astype(BF16)

    spread = dot_nt(values, cb[pl.ds(128 * nsub, 256), :])
    for i in range(2):
        scaled[nsub + i] = nsc[nsub + i] + scale[nsub + i] * spread[:, 128 * i : 128 * i + 128]

    to_upper = rcopy(scaled.at[nsub + 1], face.at[0], 8, jnp.minimum(g + 1, ngroup - 1), sub)
    to_lower = rcopy(scaled.at[nsub], face.at[1], 9, jnp.maximum(g - 1, 0), sub)

    @pl.when(g < ngroup - 1)
    def _():
        to_upper.start()

    @pl.when(g > 0)
    def _():
        to_lower.start()

    for c in range(NY):
        ty = (y + (2, 1, 3, 0)[c]) % NY
        first = ty * NZ
        spread = dot_nt(values, cb[pl.ds(pl.multiple_of(first * 128, 1024), 1024), :])
        for i in range(NZ):
            v = nsc[first + i] + scale[first + i] * spread[:, 128 * i : 128 * i + 128]
            scaled[first + i] = v
            dsend[first + i] = v.astype(BF16)

        def send_slot(o, _):
            to = first + z_at(o)
            rcopy(dsend.at[to], drecv.at[sub], 10, g, to).start()
            return 0

        lax.fori_loop(0, NZ if c < NY - 1 else NZ - 1, send_slot, 0)
    drecv[sub] = dsend[sub]

    ld_coup.wait()
    ld_dir.wait()
    ld_inner.wait()
    for k in range(ki):
        sl = pl.ds(bi * k, bi)
        quick[k] = dot(coupling[k], dirichlet[k]).astype(BF16)
        inter[:, sl] = dot(inner[:, sl].astype(BF16), dirichlet[k])

    @pl.when(g > 0)
    def _():
        to_upper.wait_recv()

    @pl.when(g == 0)
    def _():
        face[0] = jnp.zeros(face.shape[1:], F32)

    @pl.when(g < ngroup - 1)
    def _():
        to_lower.wait_recv()

    @pl.when(g == ngroup - 1)
    def _():
        face[1] = jnp.zeros(face.shape[1:], F32)

    ld_cidx.wait()
    wait_recv(drecv.at[pl.ds(0, nsub - 1)], 10)
    for j in range(slots):
        got = drecv[j].astype(F32) if j < nsub else face[j - nsub]
        v = scaled[j] + got
        iface[:, pl.ds(128 * j, 128)] = v
        picked[j] = v.astype(BF16)
    for k in range(ki):
        at = 2 * cidx[0, k]
        block = jnp.concatenate([picked[at], picked[at + 1]], axis=1)
        sl = pl.ds(bi * k, bi)
        inter[:, sl] = inter[:, sl] - dot(block, quick[k])

    wait_send(loc_all.at[pl.ds(0, NZ - 1)], 0)
    wait_send(own_all.at[pl.ds(0, NZ - 1)], 1)
    wait_send(lev.at[pl.ds(0, NY - 1)], 3)
    wait_send(lev_recv.at[pl.ds(0, NY - 1)], 4)
    wait_send(bpk.at[pl.ds(0, NZ - 1)], 2)
    wait_send(p2.at[pl.ds(0, plane - 1)], 5)
    wait_send(p3.at[pl.ds(0, NZ - 1)], 6)
    wait_send(c2.at[pl.ds(0, NY - 1)], 7)
    wait_send(npk.at[pl.ds(0, NZ - 1)], 11)

    @pl.when(g < ngroup - 1)
    def _():
        to_upper.wait_send()

    @pl.when(g > 0)
    def _():
        to_lower.wait_send()

    wait_send(drecv.at[pl.ds(0, nsub - 1)], 10)


def store(iface, inter, iface_h, inter_h, sem):
    copies = [
        pltpu.make_async_copy(iface, iface_h.at[0], sem.at[0]),
        pltpu.make_async_copy(inter, inter_h.at[0], sem.at[1]),
    ]
    for c in copies:
        c.start()
    for c in copies:
        c.wait()


def shards(
    resid_iface,
    resid_inner,
    weights,
    nbr,
    own2,
    cidx,
    neumann,
    dirichlet,
    coupling,
    coarse_basis,
    group_basis,
    group_inverse,
    top_inverse,
):
    ngroup = lax.axis_size("group")
    nsub = lax.axis_size("sub")
    rows, width = resid_iface.shape[1:]
    inner_width = resid_inner.shape[2]
    group_width = group_inverse.shape[0]
    slots = nsub + 2
    ins = (
        resid_iface[0],
        resid_inner[0],
        weights,
        nbr,
        own2,
        cidx,
        neumann[0],
        dirichlet[0],
        coupling[0],
        coarse_basis[0],
        group_basis,
        group_inverse.T,
        top_inverse,
    )
    v, s = pltpu.VMEM, pltpu.SMEM
    staged = [
        (v if i not in (3, 5) else s)(a.shape, a.dtype) for i, a in enumerate(ins) if i != 4
    ]
    work = [
        v((slots, 1, 128), F32),
        v((rows, width), BF16),
        v((NZ, rows, 128), BF16),
        v((NZ, 1, 128), jnp.int32),
        v((NZ, 32, 128), BF16),
        v((NZ, 32, 128), BF16),
        v((64 * NZ, 128), BF16),
        v((256, 128 * NZ), BF16),
        v((128, 128 * NZ), BF16),
        v((NY, rows, group_width // NY), BF16),
        v((NY, rows, group_width // NY), BF16),
        v((NY, rows, group_width // NY), BF16),
        v((group_width, 128), BF16),
        v((128, group_width), BF16),
        v((NZ, 32, 128), BF16),
        v((NZ, 32, 128), BF16),
        v((64 * NZ, 128), BF16),
        v((ngroup * NY, rows, 128), BF16),
        v((NZ, rows * NZ // 2, 128), BF16),
        v((NY, rows * NZ // 2, 128), BF16),
        v((slots, rows, 128), F32),
        v((slots, rows, 128), F32),
        v((nsub, rows, 128), BF16),
        v((nsub, rows, 128), BF16),
        v((2, rows, 128), F32),
        v((slots, rows, 128), BF16),
        v(coupling.shape[1:], BF16),
    ]
    sems = [
        pltpu.SemaphoreType.DMA((13,)),
        pltpu.SemaphoreType.DMA((12,)),
        pltpu.SemaphoreType.DMA((12,)),
    ]
    anywhere = pl.BlockSpec(memory_space=pl.ANY)
    iface, inter = pl.pallas_call(
        functools.partial(kernel, ngroup, nsub),
        out_shape=(
            pltpu.VMEM((rows, width), F32),
            pltpu.VMEM((rows, inner_width), F32),
        ),
        in_specs=[anywhere] * len(ins),
        out_specs=(pl.BlockSpec(memory_space=pltpu.VMEM),) * 2,
        scratch_shapes=staged + work + sems,
        compiler_params=pltpu.CompilerParams(
            collective_id=0, has_side_effects=True, vmem_limit_bytes=60 * 2**20
        ),
        name="bddc",
    )(*ins)
    iface, inter = pl.pallas_call(
        store,
        out_shape=(
            jax.ShapeDtypeStruct((1, rows, width), F32),
            jax.ShapeDtypeStruct((1, rows, inner_width), F32),
        ),
        in_specs=[anywhere] * 2,
        out_specs=(anywhere, anywhere),
        scratch_shapes=[pltpu.SemaphoreType.DMA((2,))],
        compiler_params=pltpu.CompilerParams(vmem_limit_bytes=2**20),
        name="store",
    )(iface, inter)
    return iface, inter


def solution(mesh):
    one = P(("group", "sub"), None)
    two = P(("group", "sub"), None, None)
    three = P(("group", "sub"), None, None, None)
    return jax.shard_map(
        shards,
        mesh=mesh,
        in_specs=(two, two, one, one, one, one, three, three, three, two, one, P("group", "sub"), P()),
        out_specs=(two, two),
        check_vma=False,
    )
```

```python
import functools

import jax
import jax.numpy as jnp
from jax import lax
from jax.experimental import pallas as pl
from jax.experimental.pallas import tpu as pltpu
from jax.sharding import PartitionSpec as P

F32 = jnp.float32
BF16 = jnp.bfloat16
MESH = pl.DeviceIdType.MESH
NT = (((1,), (1,)), ((), ()))

NY, NZ = 4, 8
QZ = NZ // 2


def dot(a, b):
    return jnp.dot(a, b, preferred_element_type=F32)


def dot_nt(a, b):
    return lax.dot_general(a, b, NT, preferred_element_type=F32)


def kernel(
    ngroup,
    nsub,
    resid_h,
    inner_h,
    weights_h,
    nbr_h,
    own_h,
    cidx_h,
    neumann_h,
    dirichlet_h,
    coupling_h,
    cb_h,
    basis_h,
    ginv_h,
    top_h,
    iface,
    inter,
    resid,
    inner,
    weights,
    nbr,
    cidx,
    neumann,
    dirichlet,
    coupling,
    cb,
    basis,
    ginv,
    top,
    scale,
    weighted,
    loc_all,
    own_all,
    bsend,
    bfull,
    ohl,
    lhs,
    lev_send,
    lev_recv,
    lev,
    ohv,
    ginv_pad,
    nsend,
    nz,
    p2,
    p3,
    c2,
    nsc,
    scaled,
    dsend,
    drecv,
    face,
    picked,
    quick,
    in_sem,
    send_sem,
    recv_sem,
):
    g = lax.axis_index("group")
    sub = lax.axis_index("sub")
    y, z = sub // NZ, sub % NZ
    par = sub % 2
    slots = nsub + 2
    kn = neumann.shape[0]
    ki = dirichlet.shape[0]
    bi = dirichlet.shape[1]

    loads = [
        (nbr_h, nbr),
        (weights_h, weights),
        (resid_h, resid),
        (cb_h, cb),
        (own_h, own_all.at[z]),
        (basis_h, basis),
        (neumann_h, neumann),
        (top_h, top),
        (ginv_h, ginv),
        (cidx_h, cidx),
        (inner_h, inner),
        (coupling_h, coupling),
        (dirichlet_h, dirichlet),
    ]
    loads = [pltpu.make_async_copy(s, d, in_sem.at[i]) for i, (s, d) in enumerate(loads)]
    (ld_nbr, ld_w, ld_resid, ld_cb, ld_own, ld_basis, ld_neu, ld_top, ld_ginv, ld_cidx, ld_inner, ld_coup, ld_dir) = loads

    def far_first(i, n):
        return n // 2 + jnp.where(i % 2 == 1, -((i + 1) // 2), i // 2)

    def z_at(i):
        return (z + far_first(i, NZ)) % NZ

    def y_at(i):
        return (y + far_first(i, NY)) % NY

    def plane_peer(o):
        tg = (g // 2 + far_first(o // (2 * NY), ngroup // 2)) % (ngroup // 2) * 2 + (g + 1 - o % 2) % 2
        return tg, y_at(o // 2 % NY) * NZ + z

    barrier = pltpu.get_barrier_semaphore()
    plane = ngroup * NY

    def greet_z(i, _):
        pl.semaphore_signal(barrier, inc=1, device_id=(g, y * NZ + z_at(i)), device_id_type=MESH)
        return 0

    def greet_plane(o, _):
        pl.semaphore_signal(barrier, inc=1, device_id=plane_peer(o), device_id_type=MESH)
        return 0

    lax.fori_loop(0, NZ - 1, greet_z, 0)
    for ld in (ld_cb, ld_resid, ld_nbr, ld_w, ld_basis, ld_own):
        ld.start()
    lax.fori_loop(0, plane - 1, greet_plane, 0)

    def rcopy(src, dst, phase, tg, ts):
        return pltpu.make_async_remote_copy(
            src_ref=src,
            dst_ref=dst,
            send_sem=send_sem.at[phase],
            recv_sem=recv_sem.at[phase],
            device_id=(tg, ts),
            device_id_type=MESH,
        )

    def wait_recv(ref, phase):
        pltpu.make_async_copy(ref, ref, recv_sem.at[phase]).wait()

    def wait_send(ref, phase):
        pltpu.make_async_copy(ref, ref, send_sem.at[phase]).wait()

    k_mine, half = z % QZ, z // QZ
    my_rows = pl.ds(pl.multiple_of(64 * z, 64), 64)
    my_nz_rows = pl.ds(pl.multiple_of(64 * k_mine, 64), 64)

    def tiles(src, dst):
        for k in range(QZ):
            dst[k] = src[:, 128 * k : 128 * k + 128].astype(BF16)

    ld_nbr.wait()
    ld_w.wait()
    ld_resid.wait()
    for j in range(slots):
        sl = pl.ds(128 * j, 128)
        sc = weights[:, sl]
        if j < nsub:
            sc = sc * nbr[0, j].astype(F32)
        scale[j] = sc
        weighted[:, sl] = (sc * resid[:, sl]).astype(BF16)
    ld_cb.wait()
    loc_all[z] = dot(weighted[...], cb[...]).astype(BF16)
    ld_basis.wait()
    tiles(basis[...], bsend)
    bfull[my_rows, :] = bsend[k_mine]
    ld_own.wait()

    for ld in (ld_top, ld_ginv, ld_neu, ld_coup, ld_dir, ld_inner, ld_cidx):
        ld.start()

    pl.semaphore_wait(barrier, NZ - 1 + plane - 1)

    def send_loc(i, _):
        tz = z_at(i)
        rcopy(own_all.at[z], own_all.at[z], 1, g, y * NZ + tz).start()
        rcopy(loc_all.at[z], loc_all.at[z], 0, g, y * NZ + tz).start()
        return 0

    lax.fori_loop(0, NZ - 1, send_loc, 0)

    def send_z(i, _):
        tz = z_at(i)
        rcopy(bsend.at[tz % QZ], bfull.at[my_rows], 2, g, y * NZ + tz).start()
        return 0

    lax.fori_loop(0, NZ - 1, send_z, 0)

    ld_top.wait()
    tiles(dot(basis[...].astype(BF16), top[...].astype(BF16)), nsend)
    nz[my_nz_rows, :] = nsend[k_mine]

    def send_n(i, _):
        k = (k_mine + i) % QZ
        rcopy(nsend.at[k], nz.at[my_nz_rows], 11, g, y * NZ + half * QZ + k).start()
        return 0

    lax.fori_loop(1, QZ, send_n, 0)
    mine_rows = pl.ds(pl.multiple_of(par * 64, 64), 64)
    other_rows = pl.ds(pl.multiple_of((1 - par) * 64, 64), 64)
    ld_ginv.wait()
    ginv_pad[mine_rows, :] = ginv[...].astype(BF16)
    ginv_pad[other_rows, :] = jnp.zeros((64, ginv.shape[1]), BF16)

    wait_recv(own_all.at[pl.ds(0, NZ - 1)], 1)
    wait_recv(loc_all.at[pl.ds(0, NZ - 1)], 0)
    count = lax.broadcasted_iota(jnp.int32, (256, 128), 0).astype(F32).astype(BF16)
    one, nil = jnp.ones((256, 128), BF16), jnp.zeros((256, 128), BF16)
    for s in range(NZ):
        at = pl.ds(128 * s, 128)
        o = own_all[s]
        lo = (o & 255).astype(F32).astype(BF16)
        hi = (o >> 8).astype(F32).astype(BF16)
        ohl[:, at] = jnp.where(count == lo, one, nil)
        v = loc_all[s]
        for h in range(8):
            lhs[pl.ds(16 * h, 16), at] = jnp.where(hi == h, v, nil[:16])
    level2 = dot_nt(lhs[...], ohl[...])
    for h in range(8):
        lev_send[h // 2, :, pl.ds(256 * (h % 2), 256)] = level2[16 * h : 16 * h + 16, :].astype(BF16)

    def send_lev(i, _):
        ty = y_at(i)
        rcopy(lev_send.at[ty], lev_recv.at[y], 4, g, ty * NZ + z).start()
        return 0

    lax.fori_loop(0, NY - 1, send_lev, 0)
    lev_recv[y] = lev_send[y]

    wait_recv(bfull.at[pl.ds(0, 64 * (NZ - 1))], 2)
    wait_recv(lev_recv.at[pl.ds(0, NY - 1)], 4)
    mine = lev_recv[0].astype(F32)
    for k in range(1, NY):
        mine = mine + lev_recv[k].astype(F32)
    lev[y] = mine.astype(BF16)
    p2[g * NY + y] = dot(lev[y], bfull[...]).astype(BF16)

    def send_plane(o, _):
        tg, ts = plane_peer(o)
        rcopy(p2.at[g * NY + y], p2.at[g * NY + y], 5, tg, ts).start()
        return 0

    lax.fori_loop(0, plane - 1, send_plane, 0)

    def send_level2(i, _):
        rcopy(lev.at[y], lev.at[y], 3, g, y_at(i) * NZ + z).start()
        return 0

    lax.fori_loop(0, NY - 1, send_level2, 0)

    ld_coup.wait()
    ld_dir.wait()
    ld_inner.wait()
    for k in range(ki):
        sl = pl.ds(bi * k, bi)
        quick[k] = dot(coupling[k], dirichlet[k]).astype(BF16)
        inter[:, sl] = dot(inner[:, sl].astype(BF16), dirichlet[k])

    wait_recv(lev.at[pl.ds(0, NY - 1)], 3)
    solved = dot_nt(jnp.concatenate([lev[k] for k in range(NY)], axis=1), ginv_pad[...])
    wait_recv(nz.at[pl.ds(0, 64 * (QZ - 1))], 11)
    wait_recv(p2.at[pl.ds(0, plane - 1)], 5)
    level3 = p2[0].astype(F32)
    for k in range(1, plane):
        level3 = level3 + p2[k].astype(F32)

    part = dot_nt(level3.astype(BF16), nz[...])
    for t in range(QZ // 2):
        own_part = jnp.where(z // 2 % 2 == t, solved, 0.0)
        p3[z, pl.ds(16 * t, 16), :] = (part[:, 128 * t : 128 * t + 128] + own_part).astype(BF16)

    def send_part(i, _):
        rcopy(p3.at[z], p3.at[z], 6, g, y * NZ + z_at(i)).start()
        return 0

    lax.fori_loop(0, NZ - 1, send_part, 0)

    def pick(t, _):
        at = pl.multiple_of(t * 256, 256)
        ohv[pl.ds(at, 256), :] = (
            (lax.broadcasted_iota(jnp.int32, (256, 128), 0) + at == own_all[z]).astype(F32).astype(BF16)
        )
        return 0

    lax.fori_loop(0, 8, pick, 0)
    wait_recv(p3.at[pl.ds(0, NZ - 1)], 6)
    for h in range(2):
        c2y = p3[QZ * h].astype(F32)
        for k in range(1, QZ):
            c2y = c2y + p3[QZ * h + k].astype(F32)
        c2[y, pl.ds(32 * h, 32), :] = c2y.astype(BF16)

    def send_coarse(i, _):
        rcopy(c2.at[y], c2.at[y], 7, g, y_at(i) * NZ + z).start()
        return 0

    lax.fori_loop(0, NY - 1, send_coarse, 0)
    ld_neu.wait()
    for k in range(kn):
        v = dot(weighted[:, 256 * k : 256 * k + 256], neumann[k])
        nsc[2 * k] = v[:, :128] * scale[2 * k]
        nsc[2 * k + 1] = v[:, 128:] * scale[2 * k + 1]
    wait_recv(c2.at[pl.ds(0, NY - 1)], 7)
    coarse2 = jnp.concatenate(
        [c2[k, 16 * t : 16 * t + 16, :] for k in range(NY) for t in range(NZ // 2)], axis=1
    )
    values = dot(coarse2, ohv[...]).astype(BF16)

    spread = dot_nt(values, cb[pl.ds(128 * nsub, 256), :])
    for i in range(2):
        scaled[nsub + i] = nsc[nsub + i] + scale[nsub + i] * spread[:, 128 * i : 128 * i + 128]

    to_upper = rcopy(scaled.at[nsub + 1], face.at[0], 8, jnp.minimum(g + 1, ngroup - 1), sub)
    to_lower = rcopy(scaled.at[nsub], face.at[1], 9, jnp.maximum(g - 1, 0), sub)

    @pl.when(g < ngroup - 1)
    def _():
        to_upper.start()

    @pl.when(g > 0)
    def _():
        to_lower.start()

    for c in range(NY):
        ty = (y + (2, 1, 3, 0)[c]) % NY
        first = ty * NZ
        spread = dot_nt(values, cb[pl.ds(pl.multiple_of(first * 128, 1024), 1024), :])
        for i in range(NZ):
            v = nsc[first + i] + scale[first + i] * spread[:, 128 * i : 128 * i + 128]
            scaled[first + i] = v
            dsend[first + i] = v.astype(BF16)

        def send_slot(o, _):
            to = first + z_at(o)
            rcopy(dsend.at[to], drecv.at[sub], 10, g, to).start()
            return 0

        lax.fori_loop(0, NZ if c < NY - 1 else NZ - 1, send_slot, 0)
    drecv[sub] = dsend[sub]


    @pl.when(g > 0)
    def _():
        to_upper.wait_recv()

    @pl.when(g == 0)
    def _():
        face[0] = jnp.zeros(face.shape[1:], F32)

    @pl.when(g < ngroup - 1)
    def _():
        to_lower.wait_recv()

    @pl.when(g == ngroup - 1)
    def _():
        face[1] = jnp.zeros(face.shape[1:], F32)

    ld_cidx.wait()
    wait_recv(drecv.at[pl.ds(0, nsub - 1)], 10)
    for j in range(slots):
        got = drecv[j].astype(F32) if j < nsub else face[j - nsub]
        v = scaled[j] + got
        iface[:, pl.ds(128 * j, 128)] = v
        picked[j] = v.astype(BF16)
    for k in range(ki):
        at = 2 * cidx[0, k]
        block = jnp.concatenate([picked[at], picked[at + 1]], axis=1)
        sl = pl.ds(bi * k, bi)
        inter[:, sl] = inter[:, sl] - dot(block, quick[k])

    wait_send(loc_all.at[pl.ds(0, NZ - 1)], 0)
    wait_send(own_all.at[pl.ds(0, NZ - 1)], 1)
    wait_send(lev.at[pl.ds(0, NY - 1)], 3)
    wait_send(lev_recv.at[pl.ds(0, NY - 1)], 4)
    wait_send(bfull.at[pl.ds(0, 64 * (NZ - 1))], 2)
    wait_send(p2.at[pl.ds(0, plane - 1)], 5)
    wait_send(p3.at[pl.ds(0, NZ - 1)], 6)
    wait_send(c2.at[pl.ds(0, NY - 1)], 7)
    wait_send(nz.at[pl.ds(0, 64 * (QZ - 1))], 11)

    @pl.when(g < ngroup - 1)
    def _():
        to_upper.wait_send()

    @pl.when(g > 0)
    def _():
        to_lower.wait_send()

    wait_send(drecv.at[pl.ds(0, nsub - 1)], 10)


def store(iface, inter, iface_h, inter_h, sem):
    copies = [
        pltpu.make_async_copy(iface, iface_h.at[0], sem.at[0]),
        pltpu.make_async_copy(inter, inter_h.at[0], sem.at[1]),
    ]
    for c in copies:
        c.start()
    for c in copies:
        c.wait()


def shards(
    resid_iface,
    resid_inner,
    weights,
    nbr,
    own2,
    cidx,
    neumann,
    dirichlet,
    coupling,
    coarse_basis,
    group_basis,
    group_inverse,
    top_inverse,
):
    ngroup = lax.axis_size("group")
    nsub = lax.axis_size("sub")
    rows, width = resid_iface.shape[1:]
    inner_width = resid_inner.shape[2]
    group_width = group_inverse.shape[0]
    slots = nsub + 2
    ins = (
        resid_iface[0],
        resid_inner[0],
        weights,
        nbr,
        own2,
        cidx,
        neumann[0],
        dirichlet[0],
        coupling[0],
        coarse_basis[0],
        group_basis,
        group_inverse.T,
        top_inverse,
    )
    v, s = pltpu.VMEM, pltpu.SMEM
    staged = [
        (v if i not in (3, 5) else s)(a.shape, a.dtype) for i, a in enumerate(ins) if i != 4
    ]
    work = [
        v((slots, 1, 128), F32),
        v((rows, width), BF16),
        v((NZ, rows, 128), BF16),
        v((NZ, 1, 128), jnp.int32),
        v((QZ, 64, 128), BF16),
        v((64 * NZ, 128), BF16),
        v((256, 128 * NZ), BF16),
        v((128, 128 * NZ), BF16),
        v((NY, rows, group_width // NY), BF16),
        v((NY, rows, group_width // NY), BF16),
        v((NY, rows, group_width // NY), BF16),
        v((group_width, 128), BF16),
        v((128, group_width), BF16),
        v((QZ, 64, 128), BF16),
        v((64 * QZ, 128), BF16),
        v((ngroup * NY, rows, 128), BF16),
        v((NZ, rows * QZ // 2, 128), BF16),
        v((NY, rows * NZ // 2, 128), BF16),
        v((slots, rows, 128), F32),
        v((slots, rows, 128), F32),
        v((nsub, rows, 128), BF16),
        v((nsub, rows, 128), BF16),
        v((2, rows, 128), F32),
        v((slots, rows, 128), BF16),
        v(coupling.shape[1:], BF16),
    ]
    sems = [
        pltpu.SemaphoreType.DMA((13,)),
        pltpu.SemaphoreType.DMA((12,)),
        pltpu.SemaphoreType.DMA((12,)),
    ]
    anywhere = pl.BlockSpec(memory_space=pl.ANY)
    iface, inter = pl.pallas_call(
        functools.partial(kernel, ngroup, nsub),
        out_shape=(
            pltpu.VMEM((rows, width), F32),
            pltpu.VMEM((rows, inner_width), F32),
        ),
        in_specs=[anywhere] * len(ins),
        out_specs=(pl.BlockSpec(memory_space=pltpu.VMEM),) * 2,
        scratch_shapes=staged + work + sems,
        compiler_params=pltpu.CompilerParams(
            collective_id=0, has_side_effects=True, vmem_limit_bytes=60 * 2**20
        ),
        name="bddc",
    )(*ins)
    iface, inter = pl.pallas_call(
        store,
        out_shape=(
            jax.ShapeDtypeStruct((1, rows, width), F32),
            jax.ShapeDtypeStruct((1, rows, inner_width), F32),
        ),
        in_specs=[anywhere] * 2,
        out_specs=(anywhere, anywhere),
        scratch_shapes=[pltpu.SemaphoreType.DMA((2,))],
        compiler_params=pltpu.CompilerParams(vmem_limit_bytes=2**20),
        name="store",
    )(iface, inter)
    return iface, inter


def solution(mesh):
    one = P(("group", "sub"), None)
    two = P(("group", "sub"), None, None)
    three = P(("group", "sub"), None, None, None)
    return jax.shard_map(
        shards,
        mesh=mesh,
        in_specs=(two, two, one, one, one, one, three, three, three, two, one, P("group", "sub"), P()),
        out_specs=(two, two),
        check_vma=False,
    )
```

```python
import functools

import jax
import jax.numpy as jnp
from jax import lax
from jax.experimental import pallas as pl
from jax.experimental.pallas import tpu as pltpu
from jax.sharding import PartitionSpec as P

F32 = jnp.float32
BF16 = jnp.bfloat16
MESH = pl.DeviceIdType.MESH
NT = (((1,), (1,)), ((), ()))

NY, NZ = 4, 8
QZ = NZ // 2


def dot(a, b):
    return jnp.dot(a, b, preferred_element_type=F32)


def dot_nt(a, b):
    return lax.dot_general(a, b, NT, preferred_element_type=F32)


def kernel(
    ngroup,
    nsub,
    resid_h,
    inner_h,
    weights_h,
    nbr_h,
    own_h,
    cidx_h,
    neumann_h,
    dirichlet_h,
    coupling_h,
    cb_h,
    basis_h,
    ginv_h,
    top_h,
    iface,
    inter,
    resid,
    inner,
    weights,
    nbr,
    cidx,
    neumann,
    dirichlet,
    coupling,
    cb,
    basis,
    ginv,
    top,
    scale,
    weighted,
    loc_all,
    own_all,
    bsend,
    bfull,
    ohl,
    lhs,
    lev_send,
    lev_recv,
    lev,
    ohv,
    ginv_pad,
    nsend,
    nz,
    p2,
    p3,
    c2,
    nsc,
    scaled,
    dsend,
    drecv,
    face,
    picked,
    quick,
    in_sem,
    send_sem,
    recv_sem,
):
    g = lax.axis_index("group")
    sub = lax.axis_index("sub")
    y, z = sub // NZ, sub % NZ
    par = sub % 2
    slots = nsub + 2
    kn = neumann.shape[0]
    ki = dirichlet.shape[0]
    bi = dirichlet.shape[1]

    loads = [
        (nbr_h, nbr),
        (weights_h, weights),
        (resid_h, resid),
        (cb_h, cb),
        (own_h, own_all.at[z]),
        (basis_h, basis),
        (neumann_h, neumann),
        (top_h, top),
        (ginv_h, ginv),
        (cidx_h, cidx),
        (inner_h, inner),
        (coupling_h, coupling),
        (dirichlet_h, dirichlet),
    ]
    loads = [pltpu.make_async_copy(s, d, in_sem.at[i]) for i, (s, d) in enumerate(loads)]
    (ld_nbr, ld_w, ld_resid, ld_cb, ld_own, ld_basis, ld_neu, ld_top, ld_ginv, ld_cidx, ld_inner, ld_coup, ld_dir) = loads

    def far_first(i, n):
        return n // 2 + jnp.where(i % 2 == 1, -((i + 1) // 2), i // 2)

    def z_at(i):
        return (z + far_first(i, NZ)) % NZ

    def y_at(i):
        return (y + far_first(i, NY)) % NY

    def plane_peer(o):
        tg = (g // 2 + far_first(o // (2 * NY), ngroup // 2)) % (ngroup // 2) * 2 + (g + 1 - o % 2) % 2
        return tg, y_at(o // 2 % NY) * NZ + z

    barrier = pltpu.get_barrier_semaphore()
    plane = ngroup * NY

    def greet_z(i, _):
        pl.semaphore_signal(barrier, inc=1, device_id=(g, y * NZ + z_at(i)), device_id_type=MESH)
        return 0

    def greet_plane(o, _):
        pl.semaphore_signal(barrier, inc=1, device_id=plane_peer(o), device_id_type=MESH)
        return 0

    lax.fori_loop(0, NZ - 1, greet_z, 0)
    for ld in (ld_cb, ld_resid, ld_nbr, ld_w, ld_basis, ld_own):
        ld.start()
    lax.fori_loop(0, plane - 1, greet_plane, 0)

    def rcopy(src, dst, phase, tg, ts):
        return pltpu.make_async_remote_copy(
            src_ref=src,
            dst_ref=dst,
            send_sem=send_sem.at[phase],
            recv_sem=recv_sem.at[phase],
            device_id=(tg, ts),
            device_id_type=MESH,
        )

    def wait_recv(ref, phase):
        pltpu.make_async_copy(ref, ref, recv_sem.at[phase]).wait()

    def wait_send(ref, phase):
        pltpu.make_async_copy(ref, ref, send_sem.at[phase]).wait()

    k_mine, half = z % QZ, z // QZ
    my_rows = pl.ds(pl.multiple_of(64 * z, 64), 64)
    my_nz_rows = pl.ds(pl.multiple_of(64 * k_mine, 64), 64)

    def tiles(src, dst):
        for k in range(QZ):
            dst[k] = src[:, 128 * k : 128 * k + 128].astype(BF16)

    ld_nbr.wait()
    ld_w.wait()
    ld_resid.wait()
    for j in range(slots):
        sl = pl.ds(128 * j, 128)
        sc = weights[:, sl]
        if j < nsub:
            sc = sc * nbr[0, j].astype(F32)
        scale[j] = sc
        weighted[:, sl] = (sc * resid[:, sl]).astype(BF16)
    ld_cb.wait()
    loc_all[z] = dot(weighted[...], cb[...]).astype(BF16)
    ld_basis.wait()
    tiles(basis[...], bsend)
    bfull[my_rows, :] = bsend[k_mine]
    ld_own.wait()

    for ld in (ld_top, ld_ginv, ld_neu, ld_coup, ld_dir, ld_inner, ld_cidx):
        ld.start()

    pl.semaphore_wait(barrier, NZ - 1 + plane - 1)

    def send_loc(i, _):
        tz = z_at(i)
        rcopy(own_all.at[z], own_all.at[z], 1, g, y * NZ + tz).start()
        rcopy(loc_all.at[z], loc_all.at[z], 0, g, y * NZ + tz).start()
        return 0

    lax.fori_loop(0, NZ - 1, send_loc, 0)

    def send_z(i, _):
        tz = z_at(i)
        rcopy(bsend.at[tz % QZ], bfull.at[my_rows], 2, g, y * NZ + tz).start()
        return 0

    lax.fori_loop(0, NZ - 1, send_z, 0)

    ld_top.wait()
    tiles(dot(basis[...].astype(BF16), top[...].astype(BF16)), nsend)
    nz[my_nz_rows, :] = nsend[k_mine]

    def send_n(i, _):
        k = (k_mine + i) % QZ
        rcopy(nsend.at[k], nz.at[my_nz_rows], 11, g, y * NZ + half * QZ + k).start()
        return 0

    lax.fori_loop(1, QZ, send_n, 0)
    mine_rows = pl.ds(pl.multiple_of(par * 64, 64), 64)
    other_rows = pl.ds(pl.multiple_of((1 - par) * 64, 64), 64)
    ld_ginv.wait()
    ginv_pad[mine_rows, :] = ginv[...].astype(BF16)
    ginv_pad[other_rows, :] = jnp.zeros((64, ginv.shape[1]), BF16)

    wait_recv(own_all.at[pl.ds(0, NZ - 1)], 1)
    wait_recv(loc_all.at[pl.ds(0, NZ - 1)], 0)
    count = lax.broadcasted_iota(jnp.int32, (256, 128), 0).astype(F32).astype(BF16)
    one, nil = jnp.ones((256, 128), BF16), jnp.zeros((256, 128), BF16)
    for s in range(NZ):
        at = pl.ds(128 * s, 128)
        o = own_all[s]
        lo = (o & 255).astype(F32).astype(BF16)
        hi = (o >> 8).astype(F32).astype(BF16)
        ohl[:, at] = jnp.where(count == lo, one, nil)
        v = loc_all[s]
        for h in range(8):
            lhs[pl.ds(16 * h, 16), at] = jnp.where(hi == h, v, nil[:16])
    level2 = dot_nt(lhs[...], ohl[...])
    for h in range(8):
        lev_send[h // 2, :, pl.ds(256 * (h % 2), 256)] = level2[16 * h : 16 * h + 16, :].astype(BF16)

    def send_lev(i, _):
        ty = y_at(i)
        rcopy(lev_send.at[ty], lev_recv.at[y], 4, g, ty * NZ + z).start()
        return 0

    lax.fori_loop(0, NY - 1, send_lev, 0)
    lev_recv[y] = lev_send[y]

    wait_recv(bfull.at[pl.ds(0, 64 * (NZ - 1))], 2)
    wait_recv(lev_recv.at[pl.ds(0, NY - 1)], 4)
    mine = lev_recv[0].astype(F32)
    for k in range(1, NY):
        mine = mine + lev_recv[k].astype(F32)
    lev[y] = mine.astype(BF16)
    p2[g * NY + y] = dot(lev[y], bfull[...]).astype(BF16)

    def send_plane(o, _):
        tg, ts = plane_peer(o)
        rcopy(p2.at[g * NY + y], p2.at[g * NY + y], 5, tg, ts).start()
        return 0

    lax.fori_loop(0, plane - 1, send_plane, 0)

    def send_level2(i, _):
        rcopy(lev.at[y], lev.at[y], 3, g, y_at(i) * NZ + z).start()
        return 0

    lax.fori_loop(0, NY - 1, send_level2, 0)

    def prepare(first, last):
        for k in range(first, last):
            sl = pl.ds(bi * k, bi)
            quick[k] = dot(coupling[k], dirichlet[k]).astype(BF16)
            inter[:, sl] = dot(inner[:, sl].astype(BF16), dirichlet[k])

    ld_coup.wait()
    ld_dir.wait()
    ld_inner.wait()
    prepare(0, ki // 4)

    wait_recv(lev.at[pl.ds(0, NY - 1)], 3)
    solved = dot_nt(jnp.concatenate([lev[k] for k in range(NY)], axis=1), ginv_pad[...])
    wait_recv(nz.at[pl.ds(0, 64 * (QZ - 1))], 11)
    wait_recv(p2.at[pl.ds(0, plane - 1)], 5)
    level3 = p2[0].astype(F32)
    for k in range(1, plane):
        level3 = level3 + p2[k].astype(F32)

    part = dot_nt(level3.astype(BF16), nz[...])
    for t in range(QZ // 2):
        own_part = jnp.where(z // 2 % 2 == t, solved, 0.0)
        p3[z, pl.ds(16 * t, 16), :] = (part[:, 128 * t : 128 * t + 128] + own_part).astype(BF16)

    def send_part(i, _):
        rcopy(p3.at[z], p3.at[z], 6, g, y * NZ + z_at(i)).start()
        return 0

    lax.fori_loop(0, NZ - 1, send_part, 0)

    def pick(t, _):
        at = pl.multiple_of(t * 256, 256)
        ohv[pl.ds(at, 256), :] = (
            (lax.broadcasted_iota(jnp.int32, (256, 128), 0) + at == own_all[z]).astype(F32).astype(BF16)
        )
        return 0

    lax.fori_loop(0, 8, pick, 0)
    prepare(ki // 4, 3 * ki // 4)
    wait_recv(p3.at[pl.ds(0, NZ - 1)], 6)
    for h in range(2):
        c2y = p3[QZ * h].astype(F32)
        for k in range(1, QZ):
            c2y = c2y + p3[QZ * h + k].astype(F32)
        c2[y, pl.ds(32 * h, 32), :] = c2y.astype(BF16)

    def send_coarse(i, _):
        rcopy(c2.at[y], c2.at[y], 7, g, y_at(i) * NZ + z).start()
        return 0

    lax.fori_loop(0, NY - 1, send_coarse, 0)
    ld_neu.wait()
    for k in range(kn):
        v = dot(weighted[:, 256 * k : 256 * k + 256], neumann[k])
        nsc[2 * k] = v[:, :128] * scale[2 * k]
        nsc[2 * k + 1] = v[:, 128:] * scale[2 * k + 1]
    prepare(3 * ki // 4, ki)
    wait_recv(c2.at[pl.ds(0, NY - 1)], 7)
    coarse2 = jnp.concatenate(
        [c2[k, 16 * t : 16 * t + 16, :] for k in range(NY) for t in range(NZ // 2)], axis=1
    )
    values = dot(coarse2, ohv[...]).astype(BF16)

    for c in range(NY):
        ty = (y + (2, 1, 3, 0)[c]) % NY
        first = ty * NZ
        spread = dot_nt(values, cb[pl.ds(pl.multiple_of(first * 128, 1024), 1024), :])
        for i in range(NZ):
            v = nsc[first + i] + scale[first + i] * spread[:, 128 * i : 128 * i + 128]
            scaled[first + i] = v
            dsend[first + i] = v.astype(BF16)

        def send_slot(o, _):
            to = first + z_at(o)
            rcopy(dsend.at[to], drecv.at[sub], 10, g, to).start()
            return 0

        lax.fori_loop(0, NZ if c < NY - 1 else NZ - 1, send_slot, 0)

    spread = dot_nt(values, cb[pl.ds(128 * nsub, 256), :])
    for i in range(2):
        scaled[nsub + i] = nsc[nsub + i] + scale[nsub + i] * spread[:, 128 * i : 128 * i + 128]

    to_upper = rcopy(scaled.at[nsub + 1], face.at[0], 8, jnp.minimum(g + 1, ngroup - 1), sub)
    to_lower = rcopy(scaled.at[nsub], face.at[1], 9, jnp.maximum(g - 1, 0), sub)

    @pl.when(g < ngroup - 1)
    def _():
        to_upper.start()

    @pl.when(g > 0)
    def _():
        to_lower.start()

    drecv[sub] = dsend[sub]


    @pl.when(g > 0)
    def _():
        to_upper.wait_recv()

    @pl.when(g == 0)
    def _():
        face[0] = jnp.zeros(face.shape[1:], F32)

    @pl.when(g < ngroup - 1)
    def _():
        to_lower.wait_recv()

    @pl.when(g == ngroup - 1)
    def _():
        face[1] = jnp.zeros(face.shape[1:], F32)

    ld_cidx.wait()
    wait_recv(drecv.at[pl.ds(0, nsub - 1)], 10)
    for j in range(slots):
        got = drecv[j].astype(F32) if j < nsub else face[j - nsub]
        v = scaled[j] + got
        iface[:, pl.ds(128 * j, 128)] = v
        picked[j] = v.astype(BF16)
    for k in range(ki):
        at = 2 * cidx[0, k]
        block = jnp.concatenate([picked[at], picked[at + 1]], axis=1)
        sl = pl.ds(bi * k, bi)
        inter[:, sl] = inter[:, sl] - dot(block, quick[k])

    wait_send(loc_all.at[pl.ds(0, NZ - 1)], 0)
    wait_send(own_all.at[pl.ds(0, NZ - 1)], 1)
    wait_send(lev.at[pl.ds(0, NY - 1)], 3)
    wait_send(lev_recv.at[pl.ds(0, NY - 1)], 4)
    wait_send(bfull.at[pl.ds(0, 64 * (NZ - 1))], 2)
    wait_send(p2.at[pl.ds(0, plane - 1)], 5)
    wait_send(p3.at[pl.ds(0, NZ - 1)], 6)
    wait_send(c2.at[pl.ds(0, NY - 1)], 7)
    wait_send(nz.at[pl.ds(0, 64 * (QZ - 1))], 11)

    @pl.when(g < ngroup - 1)
    def _():
        to_upper.wait_send()

    @pl.when(g > 0)
    def _():
        to_lower.wait_send()

    wait_send(drecv.at[pl.ds(0, nsub - 1)], 10)


def store(iface, inter, iface_h, inter_h, sem):
    copies = [
        pltpu.make_async_copy(iface, iface_h.at[0], sem.at[0]),
        pltpu.make_async_copy(inter, inter_h.at[0], sem.at[1]),
    ]
    for c in copies:
        c.start()
    for c in copies:
        c.wait()


def shards(
    resid_iface,
    resid_inner,
    weights,
    nbr,
    own2,
    cidx,
    neumann,
    dirichlet,
    coupling,
    coarse_basis,
    group_basis,
    group_inverse,
    top_inverse,
):
    ngroup = lax.axis_size("group")
    nsub = lax.axis_size("sub")
    rows, width = resid_iface.shape[1:]
    inner_width = resid_inner.shape[2]
    group_width = group_inverse.shape[0]
    slots = nsub + 2
    ins = (
        resid_iface[0],
        resid_inner[0],
        weights,
        nbr,
        own2,
        cidx,
        neumann[0],
        dirichlet[0],
        coupling[0],
        coarse_basis[0],
        group_basis,
        group_inverse.T,
        top_inverse,
    )
    v, s = pltpu.VMEM, pltpu.SMEM
    staged = [
        (v if i not in (3, 5) else s)(a.shape, a.dtype) for i, a in enumerate(ins) if i != 4
    ]
    work = [
        v((slots, 1, 128), F32),
        v((rows, width), BF16),
        v((NZ, rows, 128), BF16),
        v((NZ, 1, 128), jnp.int32),
        v((QZ, 64, 128), BF16),
        v((64 * NZ, 128), BF16),
        v((256, 128 * NZ), BF16),
        v((128, 128 * NZ), BF16),
        v((NY, rows, group_width // NY), BF16),
        v((NY, rows, group_width // NY), BF16),
        v((NY, rows, group_width // NY), BF16),
        v((group_width, 128), BF16),
        v((128, group_width), BF16),
        v((QZ, 64, 128), BF16),
        v((64 * QZ, 128), BF16),
        v((ngroup * NY, rows, 128), BF16),
        v((NZ, rows * QZ // 2, 128), BF16),
        v((NY, rows * NZ // 2, 128), BF16),
        v((slots, rows, 128), F32),
        v((slots, rows, 128), F32),
        v((nsub, rows, 128), BF16),
        v((nsub, rows, 128), BF16),
        v((2, rows, 128), F32),
        v((slots, rows, 128), BF16),
        v(coupling.shape[1:], BF16),
    ]
    sems = [
        pltpu.SemaphoreType.DMA((13,)),
        pltpu.SemaphoreType.DMA((12,)),
        pltpu.SemaphoreType.DMA((12,)),
    ]
    anywhere = pl.BlockSpec(memory_space=pl.ANY)
    iface, inter = pl.pallas_call(
        functools.partial(kernel, ngroup, nsub),
        out_shape=(
            pltpu.VMEM((rows, width), F32),
            pltpu.VMEM((rows, inner_width), F32),
        ),
        in_specs=[anywhere] * len(ins),
        out_specs=(pl.BlockSpec(memory_space=pltpu.VMEM),) * 2,
        scratch_shapes=staged + work + sems,
        compiler_params=pltpu.CompilerParams(
            collective_id=0, has_side_effects=True, vmem_limit_bytes=60 * 2**20
        ),
        name="bddc",
    )(*ins)
    iface, inter = pl.pallas_call(
        store,
        out_shape=(
            jax.ShapeDtypeStruct((1, rows, width), F32),
            jax.ShapeDtypeStruct((1, rows, inner_width), F32),
        ),
        in_specs=[anywhere] * 2,
        out_specs=(anywhere, anywhere),
        scratch_shapes=[pltpu.SemaphoreType.DMA((2,))],
        compiler_params=pltpu.CompilerParams(vmem_limit_bytes=2**20),
        name="store",
    )(iface, inter)
    return iface, inter


def solution(mesh):
    one = P(("group", "sub"), None)
    two = P(("group", "sub"), None, None)
    three = P(("group", "sub"), None, None, None)
    return jax.shard_map(
        shards,
        mesh=mesh,
        in_specs=(two, two, one, one, one, one, three, three, three, two, one, P("group", "sub"), P()),
        out_specs=(two, two),
        check_vma=False,
    )
```
